128 devices in a mesh: tp: 4 (over y_hi, core), ctx: 32 (over z, x, y_lo).
Axes of the slice: x: 4, y: 4 (y_hi: 2, y_lo: 2; y = y_hi * 2 + y_lo), z: 4, core: 2. Of those that a mesh axis runs over, the one named last changes fastest.
Arguments:
- teacher_qkv: bfloat16 [6144, 3, 1024], P('ctx', None, 'tp'), may hold values from -20 to 20
- student_qkv: bfloat16 [6144, 3, 1024], P('ctx', None, 'tp'), may hold values from -20 to 20
- segment_ids: int32 [6144], P('ctx'), may hold values from 0 to 5, never falling along the last dimension, each value on 1 to 2048 neighbouring positions
Outputs:
- loss: float32 [], replicated
- student_grad: float32 [6144, 3, 1024], P('ctx', None, 'tp')
The draws below stay inside these ranges and needn't reach their ends.
All inputs are finite; a program needn't handle non-finite values.
Results may differ from the reference program's by a relative error of at most 0.006.
Values may be sent and summed in bfloat16 or wider, within the bound.
No kernel may reach another device: no remote copies, remote signals or barrier semaphores. Data moves between devices by JAX's collectives and lax.ppermute only.
A program may use at most 128 MiB of HBM per device.

```python
import math
import jax
import jax.numpy as jnp
import numpy as np
from jax import lax

H = 8
HEAD_WIDTH = 128
TOKENS = 6144
DOCS = 6
MOST = 2048


def draw_teacher_qkv(key, part):
    key = jax.random.fold_in(key, 11)
    base_key, scale_key = jax.random.split(key, 2)
    shape = (TOKENS, 3, H * HEAD_WIDTH)
    base = jnp.clip(jax.random.normal(base_key, shape, jnp.float32), -4.0, 4.0)
    row_scale = jnp.exp(jax.random.uniform(scale_key, (TOKENS, 1, 1), jnp.float32, math.log(0.6), math.log(1.6)))
    values = base * row_scale
    return values.astype(jnp.bfloat16)


def draw_student_qkv(key, part):
    key = jax.random.fold_in(key, 23)
    base_key, scale_key = jax.random.split(key, 2)
    shape = (TOKENS, 3, H * HEAD_WIDTH)
    base = jnp.clip(jax.random.normal(base_key, shape, jnp.float32), -4.0, 4.0)
    row_scale = jnp.exp(jax.random.uniform(scale_key, (TOKENS, 1, 1), jnp.float32, math.log(0.6), math.log(1.6)))
    values = base * row_scale
    return values.astype(jnp.bfloat16)


def split_up(count, total, reach, skew):
    weights = [(1 << 20) // math.isqrt(rank ** skew) + 1 for rank in range(2, count + 1)]
    rest, given = total - reach - (count - 1), [1] * (count - 1)
    while rest > 0:
        candidates = [i for i in range(count - 1) if given[i] < reach]
        pool, budget = sum([weights[i] for i in candidates]), rest
        for i in candidates:
            extra = min(reach - given[i], max(1, budget * weights[i] // pool), rest)
            given[i] = given[i] + extra
            rest = rest - extra
    return np.array([reach] + given)


def uneven_parts(rng, count, total, bound, lean):
    if count == 2:
        one = jax.random.randint(rng, (), max(1, total - bound), min(bound, total - 1) + 1)
        return jnp.stack([one, total - one])
    tallies = jnp.asarray(split_up(count, total, bound, lean), jnp.int32)
    twos = (count - 1) // 2
    source_of, taker = tallies[1:1 + 2 * twos:2], tallies[2:2 + 2 * twos:2]
    slack = jnp.minimum(source_of - 1, bound - taker)
    shifted = jax.random.randint(jax.random.fold_in(rng, 1), (twos,), 0, 1 << 20) % (slack + 1)
    tallies = tallies.at[1:1 + 2 * twos:2].set(source_of - shifted).at[2:2 + 2 * twos:2].set(taker + shifted)
    return tallies[jax.random.permutation(jax.random.fold_in(rng, 2), count)]


def setup_inputs(seed: int = 0) -> dict:
    key_of = jax.random.split(jax.random.key(seed), 4)
    teacher_qkv = draw_teacher_qkv(jax.random.fold_in(key_of[3], 71), 0)
    student_qkv = draw_student_qkv(jax.random.fold_in(key_of[3], 71), 0)
    segment_ids = jnp.searchsorted(jnp.cumsum(uneven_parts(key_of[2], DOCS, TOKENS, MOST, 2)), jnp.arange(TOKENS), side="right").astype(jnp.int32)
    return {"teacher_qkv": teacher_qkv, "student_qkv": student_qkv, "segment_ids": segment_ids}


def masked_lse(score_matrix, pair_mask):
    top = jnp.max(jnp.where(pair_mask, score_matrix, -1e30), axis=-1)
    total = jnp.sum(jnp.where(pair_mask, jnp.exp(score_matrix - top[:, None]), 0.0), axis=-1)
    return top + jnp.log(total)


def relation(rows_t, cols_t, rows_s, cols_s, segment_ids):
    total_rows = rows_t.shape[0]
    block = math.gcd(total_rows, 512)
    scale = rows_t.shape[1] ** -0.5

    def step(carry, index):
        kl_sum, col_grad = carry
        start = (index * block).astype(jnp.int32)
        row_t = lax.dynamic_slice_in_dim(rows_t, start, block, 0)
        row_s = lax.dynamic_slice_in_dim(rows_s, start, block, 0)
        seg_block = lax.dynamic_slice_in_dim(segment_ids, start, block, 0)
        pair_mask = seg_block[:, None] == segment_ids[None, :]
        a_t = jnp.dot(row_t, cols_t.T, preferred_element_type=jnp.float32) * scale
        student_attention = jnp.dot(row_s, cols_s.T, preferred_element_type=jnp.float32) * scale
        lse_t = masked_lse(a_t, pair_mask)
        lse_s = masked_lse(student_attention, pair_mask)
        p_t = jnp.where(pair_mask, jnp.exp(a_t - lse_t[:, None]), 0.0)
        p_s = jnp.where(pair_mask, jnp.exp(student_attention - lse_s[:, None]), 0.0)
        kl_value = jnp.sum(p_t * (a_t - student_attention)) - jnp.sum(lse_t) + jnp.sum(lse_s)
        gradient_floor = (p_s - p_t).astype(jnp.bfloat16)
        row_grad = jnp.dot(gradient_floor, cols_s, preferred_element_type=jnp.float32) * scale
        col_grad = col_grad + jnp.dot(gradient_floor.T, row_s, preferred_element_type=jnp.float32) * scale
        return (kl_sum + kl_value, col_grad), row_grad

    init = (jnp.zeros((), jnp.float32), jnp.zeros(cols_s.shape, jnp.float32))
    (kl_sum, col_grad), row_blocks = lax.scan(step, init, jnp.arange(total_rows // block, dtype=jnp.int32))
    return kl_sum, row_blocks.reshape(total_rows, -1), col_grad


def reference(teacher_qkv, student_qkv, segment_ids):
    teacher = teacher_qkv.reshape(TOKENS, 3, H, HEAD_WIDTH).transpose(2, 1, 0, 3)
    student = student_qkv.reshape(TOKENS, 3, H, HEAD_WIDTH).transpose(2, 1, 0, 3)

    def per_head(pair):
        th, sh = pair
        kl_first, grad_q, col_first = relation(th[0], th[1], sh[0], sh[1], segment_ids)
        kl_second, grad_k, col_second = relation(th[1], th[1], sh[1], sh[1], segment_ids)
        kl_third, grad_v, col_third = relation(th[2], th[2], sh[2], sh[2], segment_ids)
        grads = jnp.stack([grad_q, grad_k + col_first + col_second, grad_v + col_third])
        return kl_first + kl_second + kl_third, grads

    kl_heads, grads = lax.map(per_head, (teacher, student))
    student_grad = grads.transpose(2, 1, 0, 3).reshape(TOKENS, 3, H * HEAD_WIDTH)
    return jnp.sum(kl_heads) / TOKENS, student_grad
```

```python
import functools
import math

import jax
import jax.numpy as jnp
import numpy as np
from jax import lax
from jax.experimental import pallas as pl
from jax.experimental.pallas import tpu as pltpu
from jax.sharding import PartitionSpec as P

WIDTH = 128
CTX = 32
HOME = 192
HALF = 96
LAST = 5
KTYPES = 6
SCALE = WIDTH**-0.5
LOG2E = math.log2(math.e)
C2 = SCALE * LOG2E
NEG = -1e30
NCOLS = CTX * HALF
ROWS = CTX * HALF
RB = 128
CB = 256
NBLK = ROWS // RB
PADC = NCOLS + CB
MAXT = NBLK * (NCOLS // CB + 2) + 8
IN_ROWS = 2 * (HALF + 48) + 16
OUT_ROWS = HALF + 48 + 16
F32 = jnp.float32
BF16 = jnp.bfloat16
NT = (((1,), (1,)), ((), ()))


def token_table():
    f = np.arange(ROWS)
    i, c = f % 64, f // 64
    keys = HOME * c + HALF * ((i >> 4) & 1) + (i & 15)
    i, c = f % 96, f // 96
    values = HOME * c + HALF * (i >= 48) + i % 48
    return np.stack([keys, values]).reshape(2, NBLK, RB).astype(np.int32)


def params(mib=40, **kw):
    return pltpu.CompilerParams(vmem_limit_bytes=mib * 1024 * 1024, **kw)


def pack_kernel(t_ref, s_ref, seg_ref, out_ref):
    seg = jnp.broadcast_to(seg_ref[...], (16, HOME))
    step = lax.broadcasted_iota(jnp.int32, (16, HOME), 0)
    counts = jnp.sum(jnp.where(seg < step, 1.0, 0.0), axis=1, keepdims=True)
    counts = jnp.broadcast_to(counts, (16, WIDTH)).astype(BF16)
    for d in range(CTX):
        b, g, h = d % 2, (d // 2) % 8, d // 16
        lanes = slice(h * WIDTH, (h + 1) * WIDTH)
        for k, ref in enumerate((t_ref, s_ref)):
            o = k * 144
            part = 1 if g < KTYPES else 2
            out_ref[d, o : o + HALF, :] = ref[part, HALF * b : HALF * b + HALF, lanes]
            o += HALF
            if g < KTYPES:
                out_ref[d, o : o + 16, :] = ref[0, 16 * g : 16 * g + 16, lanes]
                out_ref[d, o + 16 : o + 32, :] = ref[0, HALF + 16 * g : HALF + 16 * g + 16, lanes]
                at = HALF * (1 - b) + 16 * g
                out_ref[d, o + 32 : o + 48, :] = ref[1, at : at + 16, lanes]
            else:
                at = HALF * (1 - b) + 48 * (g - KTYPES)
                out_ref[d, o : o + 48, :] = ref[2, at : at + 48, lanes]
        out_ref[d, 288:304, :] = counts


def place():
    role = lax.axis_index("ctx")
    b = lax.rem(role, 2)
    g = lax.rem(role // 2, 8)
    return b, g, g >= KTYPES


def assemble(in_ref, colt, cols, rowt, rows, b, g, is_v):
    pad = jnp.zeros((CB, WIDTH), BF16)
    colt[NCOLS:, :] = pad
    cols[NCOLS:, :] = pad

    def m16(x):
        return pl.multiple_of(x, 16)

    def columns(c, _):
        colt[pl.ds(m16(c * HALF), HALF), :] = in_ref[c, 0:HALF, :]
        cols[pl.ds(m16(c * HALF), HALF), :] = in_ref[c, 144 : 144 + HALF, :]
        return 0

    lax.fori_loop(0, CTX, columns, 0)

    @pl.when(jnp.logical_not(is_v))
    def _():
        def one(c, _):
            for o, dst in ((0, rowt), (144, rows)):
                r = c * 64
                dst[pl.ds(m16(r), 32), :] = in_ref[c, o + 96 : o + 128, :]
                dst[pl.ds(m16(r + 32 + 16 * (1 - b)), 16), :] = in_ref[c, o + 128 : o + 144, :]
                dst[pl.ds(m16(r + 32 + 16 * b), 16), :] = in_ref[c, pl.ds(m16(o + 16 * g), 16), :]
            return 0

        lax.fori_loop(0, CTX, one, 0)

    @pl.when(is_v)
    def _():
        gv = g - KTYPES

        def one(c, _):
            for o, dst in ((0, rowt), (144, rows)):
                r = c * 96
                dst[pl.ds(m16(r + 48 * (1 - b)), 48), :] = in_ref[c, o + 96 : o + 144, :]
                dst[pl.ds(m16(r + 48 * b), 48), :] = in_ref[c, pl.ds(m16(o + 48 * gv), 48), :]
            return 0

        lax.fori_loop(0, CTX, one, 0)


def documents(in_ref, b):
    total = jnp.sum(in_ref[:, 288:304, :].astype(F32), axis=0)
    starts, firsts = [], []
    for d in range(1, LAST + 1):
        t = jnp.max(total[d : d + 1, :]).astype(jnp.int32)
        home = t // HOME
        starts.append(t)
        firsts.append(home * HALF + jnp.clip(t - home * HOME - HALF * b, 0, HALF))
    return starts, firsts


def bounds(token, starts, firsts):
    lo = jnp.zeros_like(token)
    hi = jnp.full_like(token, NCOLS)
    for t, c in zip(starts, firsts):
        lo = jnp.where(token >= t, c, lo)
    for t, c in reversed(list(zip(starts, firsts))):
        hi = jnp.where(token < t, c, hi)
    return lo, hi


def list_tiles(tab_ref, lo_ref, hi_ref, tblk, tcol, tbase, starts, firsts, g, is_v):
    token = jnp.where(is_v, tab_ref[1] + 48 * (g - KTYPES), tab_ref[0] + 16 * g)
    lo, hi = bounds(token, starts, firsts)
    lo_ref[...] = lo
    hi_ref[...] = hi
    homes = RB // 64

    def value_token(f):
        c = f // 96
        i = f - c * 96
        return HOME * c + jnp.where(i >= 48, i + 48, i) + 48 * (g - KTYPES)

    def block(blk, count):
        first = jnp.where(is_v, value_token(blk * RB), HOME * homes * blk + 16 * g)
        last = jnp.where(
            is_v, value_token(blk * RB + RB - 1), HOME * (homes * blk + homes - 1) + HALF + 16 * g + 15
        )
        c0, _ = bounds(first, starts, firsts)
        _, c1 = bounds(last, starts, firsts)
        c0 = (c0 // 128) * 128
        turns = (c1 - c0 + CB - 1) // CB

        def put(k, count):
            tblk[count] = blk
            tcol[count] = c0 + k * CB
            tbase[count] = c0 + k * CB
            return count + 1

        return lax.fori_loop(0, turns, put, count)

    blocks = jnp.where(is_v, NBLK, CTX * 64 // RB)
    count = lax.fori_loop(0, blocks, block, 0)
    tblk[count] = 0
    tcol[count] = 0
    tbase[count] = 1 << 20
    return count


def tile_scores(tile, refs):
    colt, cols, rowt, rows, lo_ref, hi_ref, tblk, tcol, tbase = refs
    blk, col, base = tblk[tile], pl.multiple_of(tcol[tile], 128), tbase[tile]
    rsl = pl.ds(pl.multiple_of(blk * RB, RB), RB)
    csl = pl.ds(col, CB)
    dt = lax.dot_general(colt[csl, :], rowt[rsl, :], NT, preferred_element_type=F32)
    ds = lax.dot_general(cols[csl, :], rows[rsl, :], NT, preferred_element_type=F32)
    at = lax.broadcasted_iota(jnp.int32, (CB, RB), 0)
    lo = lo_ref[pl.ds(blk, 1), :] - base
    hi = hi_ref[pl.ds(blk, 1), :] - base
    mask = (at >= lo) & (at < hi)
    return blk, csl, rsl, dt, ds, mask


def stats_kernel(
    in_ref, tab_ref, out_ref, colt, cols, rowt, rows, lo_ref, hi_ref, mt, st, ms, ss, wt, tblk, tcol, tbase
):
    b, g, is_v = place()
    assemble(in_ref, colt, cols, rowt, rows, b, g, is_v)
    starts, firsts = documents(in_ref, b)
    count = list_tiles(tab_ref, lo_ref, hi_ref, tblk, tcol, tbase, starts, firsts, g, is_v)
    mt[...] = jnp.full(mt.shape, NEG, F32)
    ms[...] = jnp.full(ms.shape, NEG, F32)
    for ref in (st, ss, wt):
        ref[...] = jnp.zeros(ref.shape, F32)
    refs = (colt, cols, rowt, rows, lo_ref, hi_ref, tblk, tcol, tbase)

    def one(tile):
        blk, _, _, dt, ds, mask = tile_scores(tile, refs)
        dt = jnp.where(mask, dt, NEG).reshape(CB // 8, 8, RB)
        ds = jnp.where(mask, ds, NEG).reshape(CB // 8, 8, RB)
        old_t, old_s = mt[blk], ms[blk]
        new_t = jnp.maximum(old_t, jnp.max(dt, axis=0))
        new_s = jnp.maximum(old_s, jnp.max(ds, axis=0))
        et = jnp.exp2((dt - new_t[None]) * C2)
        es = jnp.exp2((ds - new_s[None]) * C2)
        decay_t = jnp.exp2((old_t - new_t) * C2)
        decay_s = jnp.exp2((old_s - new_s) * C2)
        st[blk] = st[blk] * decay_t + jnp.sum(et, axis=0)
        ss[blk] = ss[blk] * decay_s + jnp.sum(es, axis=0)
        wt[blk] = wt[blk] * decay_t + jnp.sum(et * (dt - ds), axis=0)
        mt[blk] = new_t
        ms[blk] = new_s

    def pair(i, _):
        one(2 * i)
        one(2 * i + 1)
        return 0

    lax.fori_loop(0, (count + 1) // 2, pair, 0)

    def finish(blk, _):
        m_t, m_s = mt[blk], ms[blk]
        top_t = jnp.max(m_t, axis=0, keepdims=True)
        top_s = jnp.max(m_s, axis=0, keepdims=True)
        ft = jnp.exp2((m_t - top_t) * C2)
        fs = jnp.exp2((m_s - top_s) * C2)
        sum_t = jnp.sum(st[blk] * ft, axis=0, keepdims=True)
        sum_s = jnp.sum(ss[blk] * fs, axis=0, keepdims=True)
        sum_w = jnp.sum(wt[blk] * ft, axis=0, keepdims=True)
        out_ref[blk] = jnp.concatenate(
            [top_t, sum_t, top_s, sum_s, sum_w, jnp.zeros((3, RB), F32)], axis=0
        )
        return 0

    lax.fori_loop(0, NBLK, finish, 0)


def grads_kernel(
    in_ref, tab_ref, mine_ref, other_ref, out_ref,
    colt, cols, rowt, rows, lo_ref, hi_ref, keyt, lset, lses, cg, rgt, rgf, tblk, tcol, tbase,
):
    b, g, is_v = place()
    assemble(in_ref, colt, cols, rowt, rows, b, g, is_v)
    starts, firsts = documents(in_ref, b)
    count = list_tiles(tab_ref, lo_ref, hi_ref, tblk, tcol, tbase, starts, firsts, g, is_v)
    blocks = jnp.where(is_v, NBLK, CTX * 64 // RB)

    def turn(k, _):
        at = pl.multiple_of(k * 128, 128)
        keyt[:, pl.ds(at, 128)] = cols[pl.ds(at, 128), :].T
        return 0

    lax.fori_loop(0, PADC // 128, turn, 0)
    cg[...] = jnp.zeros(cg.shape, F32)
    rgt[...] = jnp.zeros(rgt.shape, F32)

    def combine(blk, kl):
        x, y = mine_ref[blk], other_ref[blk]
        top_t = jnp.maximum(x[0:1], y[0:1])
        top_s = jnp.maximum(x[2:3], y[2:3])
        ft, gt = jnp.exp2((x[0:1] - top_t) * C2), jnp.exp2((y[0:1] - top_t) * C2)
        fs, gs = jnp.exp2((x[2:3] - top_s) * C2), jnp.exp2((y[2:3] - top_s) * C2)
        sum_t = x[1:2] * ft + y[1:2] * gt
        sum_s = x[3:4] * fs + y[3:4] * gs
        sum_w = x[4:5] * ft + y[4:5] * gt
        lse_t = top_t * C2 + jnp.log2(sum_t)
        lse_s = top_s * C2 + jnp.log2(sum_s)
        lset[pl.ds(blk, 1), :] = lse_t
        lses[pl.ds(blk, 1), :] = lse_s
        return kl + (sum_w / sum_t * SCALE + (lse_s - lse_t) * (1.0 / LOG2E))

    kl = lax.fori_loop(0, blocks, combine, jnp.zeros((1, RB), F32))
    kl = jnp.full((1, WIDTH), 0.5, F32) * jnp.sum(kl)
    high = kl.astype(BF16)
    rest = kl - high.astype(F32)
    mid = rest.astype(BF16)
    low = (rest - mid.astype(F32)).astype(BF16)
    row = lax.broadcasted_iota(jnp.int32, (16, WIDTH), 0)
    pieces = jnp.where(
        row == 0, high.astype(F32), jnp.where(row == 1, mid.astype(F32), jnp.where(row == 2, low.astype(F32), 0.0))
    ).astype(BF16)
    refs = (colt, cols, rowt, rows, lo_ref, hi_ref, tblk, tcol, tbase)

    def one(tile):
        blk, csl, rsl, dt, ds, mask = tile_scores(tile, refs)
        pt = jnp.exp2(dt * C2 - lset[pl.ds(blk, 1), :])
        ps = jnp.exp2(ds * C2 - lses[pl.ds(blk, 1), :])
        diff = jnp.where(mask, ps - pt, 0.0).astype(BF16)
        cg[csl, :] += jnp.dot(diff, rows[rsl, :], preferred_element_type=F32)
        rgt[blk] += jnp.dot(keyt[:, csl], diff, preferred_element_type=F32)

    def pair(i, _):
        one(2 * i)
        one(2 * i + 1)
        return 0

    lax.fori_loop(0, (count + 1) // 2, pair, 0)

    def back(blk, _):
        rgf[pl.ds(pl.multiple_of(blk * RB, RB), RB), :] = rgt[blk].T
        return 0

    lax.fori_loop(0, blocks, back, 0)

    def m16(x):
        return pl.multiple_of(x, 16)

    @pl.when(jnp.logical_not(is_v))
    def _():
        def one_home(c, _):
            r = c * 64
            cg[pl.ds(m16(c * HALF + 16 * g), 16), :] += rgf[pl.ds(m16(r + 32 + 16 * b), 16), :]
            out_ref[c, 96:128, :] = (rgf[pl.ds(m16(r), 32), :] * SCALE).astype(BF16)
            out_ref[c, 128:144, :] = (rgf[pl.ds(m16(r + 32 + 16 * (1 - b)), 16), :] * SCALE).astype(BF16)
            return 0

        lax.fori_loop(0, CTX, one_home, 0)

    @pl.when(is_v)
    def _():
        gv = g - KTYPES

        def one_home(c, _):
            r = c * 96
            cg[pl.ds(m16(c * HALF + 48 * gv), 48), :] += rgf[pl.ds(m16(r + 48 * b), 48), :]
            out_ref[c, 96:144, :] = (rgf[pl.ds(m16(r + 48 * (1 - b)), 48), :] * SCALE).astype(BF16)
            return 0

        lax.fori_loop(0, CTX, one_home, 0)

    def columns(c, _):
        out_ref[c, 0:HALF, :] = (cg[pl.ds(m16(c * HALF), HALF), :] * SCALE).astype(BF16)
        out_ref[c, 144:160, :] = pieces
        return 0

    lax.fori_loop(0, CTX, columns, 0)


def sum_kernel(in_ref, out_ref, loss_ref):
    def at(h, g, b):
        return (h * 8 + g) * 2 + b

    def part(d, lo, n):
        return in_ref[d, lo : lo + n, :].astype(F32)

    for h in range(2):
        lanes = slice(h * WIDTH, (h + 1) * WIDTH)
        for g in range(KTYPES):
            q = part(at(h, g, 0), 96, 32) + part(at(h, g, 1), 96, 32)
            out_ref[0, 16 * g : 16 * g + 16, lanes] = q[:16]
            out_ref[0, HALF + 16 * g : HALF + 16 * g + 16, lanes] = q[16:]
        for b in range(2):
            for g in range(KTYPES):
                own = part(at(h, g, 1 - b), 128, 16)
                for k in range(KTYPES):
                    own += part(at(h, k, b), 16 * g, 16)
                out_ref[1, HALF * b + 16 * g : HALF * b + 16 * g + 16, lanes] = own
            for v in range(2):
                own = part(at(h, KTYPES + v, 1 - b), 96, 48)
                for k in range(2):
                    own += part(at(h, KTYPES + k, b), 48 * v, 48)
                out_ref[2, HALF * b + 48 * v : HALF * b + 48 * v + 48, lanes] = own
    total = jnp.zeros((16, WIDTH), F32)
    for d in range(CTX):
        total += part(d, 144, 16)
    loss_ref[...] = jnp.sum(total, axis=0, keepdims=True)


def shards(teacher_qkv, student_qkv, segment_ids):
    teacher = jnp.transpose(teacher_qkv, (1, 0, 2))
    student = jnp.transpose(student_qkv, (1, 0, 2))
    table = jnp.asarray(token_table())
    packed = pl.pallas_call(
        pack_kernel,
        out_shape=jax.ShapeDtypeStruct((CTX, IN_ROWS, WIDTH), BF16),
        compiler_params=params(),
        name="pack",
    )(teacher, student, segment_ids.reshape(1, HOME))
    held = lax.all_to_all(packed, "ctx", 0, 0, tiled=True)

    flat = lambda n: pltpu.VMEM((n, WIDTH), BF16)
    common = [
        flat(PADC), flat(PADC), flat(ROWS), flat(ROWS),
        pltpu.VMEM((NBLK, RB), jnp.int32), pltpu.VMEM((NBLK, RB), jnp.int32),
    ]
    lists = [pltpu.SMEM((MAXT,), jnp.int32)] * 3
    state = pltpu.VMEM((NBLK, 8, RB), F32)
    stats = pl.pallas_call(
        stats_kernel,
        out_shape=jax.ShapeDtypeStruct((NBLK, 8, RB), F32),
        scratch_shapes=common + [state] * 5 + lists,
        compiler_params=params(),
        name="stats",
    )(held, table)
    other = lax.ppermute(stats, "ctx", [(i, i ^ 1) for i in range(CTX)])
    terms = pl.pallas_call(
        grads_kernel,
        out_shape=jax.ShapeDtypeStruct((CTX, OUT_ROWS, WIDTH), BF16),
        scratch_shapes=common
        + [
            pltpu.VMEM((WIDTH, PADC), BF16),
            pltpu.VMEM((NBLK, RB), F32),
            pltpu.VMEM((NBLK, RB), F32),
            pltpu.VMEM((PADC, WIDTH), F32),
            pltpu.VMEM((NBLK, WIDTH, RB), F32),
            pltpu.VMEM((ROWS, WIDTH), F32),
        ]
        + lists,
        compiler_params=params(),
        name="grads",
    )(held, table, stats, other)
    back = lax.all_to_all(terms, "ctx", 0, 0, tiled=True)
    grad, loss = pl.pallas_call(
        sum_kernel,
        out_shape=(
            jax.ShapeDtypeStruct((3, HOME, 2 * WIDTH), F32),
            jax.ShapeDtypeStruct((1, WIDTH), F32),
        ),
        compiler_params=params(),
        name="home_sum",
    )(back)
    loss = lax.psum(loss[0, 0], "tp") / (CTX * HOME)
    return loss, jnp.transpose(grad, (1, 0, 2))


def solution(mesh):
    return jax.shard_map(
        shards,
        mesh=mesh,
        in_specs=(P("ctx", None, "tp"), P("ctx", None, "tp"), P("ctx")),
        out_specs=(P(), P("ctx", None, "tp")),
        check_vma=False,
    )
```

```python
import functools
import math

import jax
import jax.numpy as jnp
from jax import lax
from jax.experimental import pallas as pl
from jax.experimental.pallas import tpu as pltpu
from jax.sharding import PartitionSpec as P

WIDTH = 128
CTX = 32
HOME = 192
HALF = 96
LAST = 5
KTYPES = 6
SCALE = WIDTH**-0.5
LOG2E = math.log2(math.e)
C2 = SCALE * LOG2E
FAR = 2.0**100
NCOLS = CTX * HALF
ROWS = CTX * HALF
RB = 256
CB = 256
NBLK = ROWS // RB
PADC = NCOLS + 256
UNROLL = 2
MAXT = NBLK * (NCOLS // CB + 2) + 8
IN_ROWS = 2 * (HALF + 48) + 16
OUT_ROWS = HALF + 48 + 16
F32 = jnp.float32
BF16 = jnp.bfloat16
NT = (((1,), (1,)), ((), ()))


def params(mib=24, **kw):
    return pltpu.CompilerParams(vmem_limit_bytes=mib * 1024 * 1024, **kw)


def pack_kernel(t_hbm, s_hbm, seg_hbm, out_ref, t_ref, s_ref, seg_ref, sems):
    copies = [
        pltpu.make_async_copy(src, dst, sems.at[k])
        for k, (src, dst) in enumerate(((t_hbm, t_ref), (s_hbm, s_ref), (seg_hbm, seg_ref)))
    ]
    for copy in copies:
        copy.start()
    for copy in copies:
        copy.wait()
    seg = jnp.broadcast_to(seg_ref[...], (16, HOME))
    step = lax.broadcasted_iota(jnp.int32, (16, HOME), 0)
    counts = jnp.sum(jnp.where(seg < step, 1.0, 0.0), axis=1, keepdims=True)
    counts = jnp.broadcast_to(counts, (16, WIDTH)).astype(BF16)
    for d in range(CTX):
        b, g, h = d % 2, (d // 2) % 8, d // 16
        lanes = slice(h * WIDTH, (h + 1) * WIDTH)
        for k, ref in enumerate((t_ref, s_ref)):
            o = k * 144
            part = 1 if g < KTYPES else 2
            out_ref[d, o : o + HALF, :] = ref[part, HALF * b : HALF * b + HALF, lanes]
            o += HALF
            if g < KTYPES:
                out_ref[d, o : o + 16, :] = ref[0, 16 * g : 16 * g + 16, lanes]
                out_ref[d, o + 16 : o + 32, :] = ref[0, HALF + 16 * g : HALF + 16 * g + 16, lanes]
                at = HALF * (1 - b) + 16 * g
                out_ref[d, o + 32 : o + 48, :] = ref[1, at : at + 16, lanes]
            else:
                at = HALF * (1 - b) + 48 * (g - KTYPES)
                out_ref[d, o : o + 48, :] = ref[2, at : at + 48, lanes]
        out_ref[d, 288:304, :] = counts


def place():
    role = lax.axis_index("ctx")
    b = lax.rem(role, 2)
    g = lax.rem(role // 2, 8)
    return b, g, g >= KTYPES


def m16(x):
    return pl.multiple_of(x, 16)


def assemble(in_ref, colt, cols, rowt, rows, b, g, is_v):
    pad = jnp.zeros((PADC - NCOLS, WIDTH), BF16)
    colt[NCOLS:, :] = pad
    cols[NCOLS:, :] = pad

    def columns(c, _):
        colt[pl.ds(m16(c * HALF), HALF), :] = in_ref[c, 0:HALF, :]
        cols[pl.ds(m16(c * HALF), HALF), :] = in_ref[c, 144 : 144 + HALF, :]
        return 0

    lax.fori_loop(0, CTX, columns, 0)

    @pl.when(jnp.logical_not(is_v))
    def _():
        def one(c, _):
            for o, dst in ((0, rowt), (144, rows)):
                r = c * 64
                dst[pl.ds(m16(r), 32), :] = in_ref[c, o + 96 : o + 128, :]
                dst[pl.ds(m16(r + 32 + 16 * (1 - b)), 16), :] = in_ref[c, o + 128 : o + 144, :]
                dst[pl.ds(m16(r + 32 + 16 * b), 16), :] = in_ref[c, pl.ds(m16(o + 16 * g), 16), :]
            return 0

        lax.fori_loop(0, CTX, one, 0)

    @pl.when(is_v)
    def _():
        gv = g - KTYPES

        def one(c, _):
            for o, dst in ((0, rowt), (144, rows)):
                r = c * 96
                dst[pl.ds(m16(r + 48 * (1 - b)), 48), :] = in_ref[c, o + 96 : o + 144, :]
                dst[pl.ds(m16(r + 48 * b), 48), :] = in_ref[c, pl.ds(m16(o + 48 * gv), 48), :]
            return 0

        lax.fori_loop(0, CTX, one, 0)


def documents(in_ref, b):
    total = jnp.sum(in_ref[:, 288:304, :].astype(F32), axis=0)
    starts, firsts = [], []
    for d in range(1, LAST + 1):
        t = jnp.max(total[d : d + 1, :]).astype(jnp.int32)
        home = t // HOME
        starts.append(t)
        firsts.append(home * HALF + jnp.clip(t - home * HOME - HALF * b, 0, HALF))
    return starts, firsts


def marks(featc, featr, starts, firsts, g, is_v):
    lane = lax.broadcasted_iota(jnp.int32, (1, WIDTH), 1)

    def edges(points, rest_lo, rest_hi):
        lo = jnp.full((1, WIDTH), rest_lo, jnp.int32)
        hi = jnp.full((1, WIDTH), rest_hi, jnp.int32)
        for s in range(len(points) - 1):
            lo = jnp.where(lane == s, points[s], lo)
            hi = jnp.where(lane == s, points[s + 1], hi)
        return lo, hi

    lo, hi = edges([0, *firsts, NCOLS, PADC], 0, 0)
    at = lax.broadcasted_iota(jnp.int32, (128, WIDTH), 0)

    def column_block(k, _):
        j = at + k * 128
        inside = (j >= lo) & (j < hi)
        featc[pl.ds(pl.multiple_of(k * 128, 128), 128), :] = jnp.where(inside, 1.0, 0.0).astype(BF16)
        return 0

    lax.fori_loop(0, PADC // 128, column_block, 0)
    tokens = CTX * HOME
    row_lo, row_hi = edges([0, *starts, tokens], -1, 2 * tokens)
    row_lo = jnp.where(lane == LAST + 1, 2 * tokens, row_lo)

    def row_block(n, first):
        def one(c, _):
            token = first + c * HOME
            inside = (token >= row_lo) & (token < row_hi)
            featr[pl.ds(m16(c * n), n), :] = jnp.where(inside, 0.0, -FAR).astype(BF16)
            return 0

        lax.fori_loop(0, CTX, one, 0)

    @pl.when(jnp.logical_not(is_v))
    def _():
        i = lax.broadcasted_iota(jnp.int32, (64, WIDTH), 0)
        row_block(64, HALF * ((i >> 4) & 1) + (i & 15) + 16 * g)

    @pl.when(is_v)
    def _():
        i = lax.broadcasted_iota(jnp.int32, (96, WIDTH), 0)
        row_block(96, i + jnp.where(i >= 48, 48, 0) + 48 * (g - KTYPES))


def list_tiles(tblk, tcol, starts, firsts, g, is_v):
    homes = RB // 64

    def value_token(f):
        c = f // 96
        i = f - c * 96
        return HOME * c + jnp.where(i >= 48, i + 48, i) + 48 * (g - KTYPES)

    def block(blk, count):
        first = jnp.where(is_v, value_token(blk * RB), HOME * homes * blk + 16 * g)
        last = jnp.where(
            is_v, value_token(blk * RB + RB - 1), HOME * (homes * blk + homes - 1) + HALF + 16 * g + 15
        )
        c0, c1 = 0, NCOLS
        for t, c in zip(starts, firsts):
            c0 = jnp.where(first >= t, c, c0)
        for t, c in reversed(list(zip(starts, firsts))):
            c1 = jnp.where(last < t, c, c1)
        c0 = lax.shift_left(lax.shift_right_logical(c0, 7), 7)

        def put(c, count):
            tblk[count] = blk
            tcol[count] = c
            return c + CB, count + 1

        _, count = lax.while_loop(lambda s: s[0] < c1, lambda s: put(*s), (c0, count))
        return count

    blocks = jnp.where(is_v, NBLK, CTX * 64 // RB)
    count = lax.fori_loop(0, blocks, block, 0)
    for k in range(UNROLL - 1):
        tblk[count + k] = 0
        tcol[count + k] = NCOLS
    return count


def tile_scores(tile, refs):
    colt, cols, rowt, rows, featc, featr, tblk, tcol = refs
    blk, col = tblk[tile], pl.multiple_of(tcol[tile], 128)
    rsl = pl.ds(pl.multiple_of(blk * RB, RB), RB)
    csl = pl.ds(col, CB)

    def score(c_ref, r_ref):
        left = jnp.concatenate([c_ref[csl, :], featc[csl, :]], axis=1)
        right = jnp.concatenate([r_ref[rsl, :], featr[rsl, :]], axis=1)
        return lax.dot_general(left, right, NT, preferred_element_type=F32)

    return blk, csl, rsl, score(colt, rowt), score(cols, rows)


def run_tiles(one, count):
    def turn(i, _):
        for k in range(UNROLL):
            one(UNROLL * i + k)
        return 0

    lax.fori_loop(0, (count + UNROLL - 1) // UNROLL, turn, 0)


def stats_kernel(
    in_ref, out_ref, colt, cols, rowt, rows, featc, featr, mt, st, ms, ss, wt, tblk, tcol
):
    b, g, is_v = place()
    starts, firsts = documents(in_ref, b)
    assemble(in_ref, colt, cols, rowt, rows, b, g, is_v)
    marks(featc, featr, starts, firsts, g, is_v)
    count = list_tiles(tblk, tcol, starts, firsts, g, is_v)
    mt[...] = jnp.full(mt.shape, -FAR, F32)
    ms[...] = jnp.full(ms.shape, -FAR, F32)
    for ref in (st, ss, wt):
        ref[...] = jnp.zeros(ref.shape, F32)
    refs = (colt, cols, rowt, rows, featc, featr, tblk, tcol)

    def one(tile):
        blk, _, _, dt, ds = tile_scores(tile, refs)
        dt = dt.reshape(CB // 8, 8, RB)
        ds = ds.reshape(CB // 8, 8, RB)
        old_t, old_s = mt[blk], ms[blk]
        new_t = jnp.maximum(old_t, jnp.max(dt, axis=0))
        new_s = jnp.maximum(old_s, jnp.max(ds, axis=0))
        et = jnp.exp2((dt - new_t[None]) * C2)
        es = jnp.exp2((ds - new_s[None]) * C2)
        decay_t = jnp.exp2((old_t - new_t) * C2)
        decay_s = jnp.exp2((old_s - new_s) * C2)
        st[blk] = st[blk] * decay_t + jnp.sum(et, axis=0)
        ss[blk] = ss[blk] * decay_s + jnp.sum(es, axis=0)
        wt[blk] = wt[blk] * decay_t + jnp.sum(et * (dt - ds), axis=0)
        mt[blk] = new_t
        ms[blk] = new_s

    run_tiles(one, count)
    out_ref[...] = jnp.zeros(out_ref.shape, F32)
    for blk in range(NBLK):
        m_t, m_s = mt[blk], ms[blk]
        top_t = jnp.max(m_t, axis=0, keepdims=True)
        top_s = jnp.max(m_s, axis=0, keepdims=True)
        ft = jnp.exp2((m_t - top_t) * C2)
        fs = jnp.exp2((m_s - top_s) * C2)
        out_ref[0, blk : blk + 1, :] = top_t
        out_ref[1, blk : blk + 1, :] = jnp.sum(st[blk] * ft, axis=0, keepdims=True)
        out_ref[2, blk : blk + 1, :] = top_s
        out_ref[3, blk : blk + 1, :] = jnp.sum(ss[blk] * fs, axis=0, keepdims=True)
        out_ref[4, blk : blk + 1, :] = jnp.sum(wt[blk] * ft, axis=0, keepdims=True)


def turn_kernel(cols, keyt):
    for k in range(PADC // 128):
        keyt[:, k * 128 : k * 128 + 128] = cols[k * 128 : k * 128 + 128, :].T


def grads_kernel(
    in_ref, colt, cols, rowt, rows, featc, featr, keyt, mine_ref, other_ref, out_ref,
    lset, lses, cg, rgt, rgf, tblk, tcol,
):
    b, g, is_v = place()
    starts, firsts = documents(in_ref, b)
    count = list_tiles(tblk, tcol, starts, firsts, g, is_v)
    blocks = jnp.where(is_v, NBLK, CTX * 64 // RB)
    cg[...] = jnp.zeros(cg.shape, F32)
    rgt[...] = jnp.zeros(rgt.shape, F32)

    top_t = jnp.maximum(mine_ref[0], other_ref[0])
    top_s = jnp.maximum(mine_ref[2], other_ref[2])
    sum_t, sum_s, sum_w = 0.0, 0.0, 0.0
    for ref in (mine_ref, other_ref):
        ft = jnp.exp2((ref[0] - top_t) * C2)
        fs = jnp.exp2((ref[2] - top_s) * C2)
        sum_t += ref[1] * ft
        sum_s += ref[3] * fs
        sum_w += ref[4] * ft
    lse_t = top_t * C2 + jnp.log2(sum_t)
    lse_s = top_s * C2 + jnp.log2(sum_s)
    lset[...] = lse_t
    lses[...] = lse_s
    kl = sum_w / sum_t * SCALE + (lse_s - lse_t) * (1.0 / LOG2E)
    used = lax.broadcasted_iota(jnp.int32, kl.shape, 0) < blocks
    kl = jnp.full((1, WIDTH), 0.5, F32) * jnp.sum(jnp.where(used, kl, 0.0))
    high = kl.astype(BF16)
    rest = kl - high.astype(F32)
    mid = rest.astype(BF16)
    low = (rest - mid.astype(F32)).astype(BF16)
    row = lax.broadcasted_iota(jnp.int32, (16, WIDTH), 0)
    pieces = jnp.where(
        row == 0, high.astype(F32), jnp.where(row == 1, mid.astype(F32), jnp.where(row == 2, low.astype(F32), 0.0))
    ).astype(BF16)
    refs = (colt, cols, rowt, rows, featc, featr, tblk, tcol)

    def one(tile):
        blk, csl, rsl, dt, ds = tile_scores(tile, refs)
        pt = jnp.exp2(dt * C2 - lset[pl.ds(blk, 1), :])
        ps = jnp.exp2(ds * C2 - lses[pl.ds(blk, 1), :])
        diff = (ps - pt).astype(BF16)
        cg[csl, :] += jnp.dot(diff, rows[rsl, :], preferred_element_type=F32)
        rgt[blk] += jnp.dot(keyt[:, csl], diff, preferred_element_type=F32)

    run_tiles(one, count)

    for blk in range(NBLK):
        rgf[blk * RB : blk * RB + RB, :] = rgt[blk].T

    @pl.when(jnp.logical_not(is_v))
    def _():
        def one_home(c, _):
            r = c * 64
            cg[pl.ds(m16(c * HALF + 16 * g), 16), :] += rgf[pl.ds(m16(r + 32 + 16 * b), 16), :]
            out_ref[c, 96:128, :] = (rgf[pl.ds(m16(r), 32), :] * SCALE).astype(BF16)
            out_ref[c, 128:144, :] = (rgf[pl.ds(m16(r + 32 + 16 * (1 - b)), 16), :] * SCALE).astype(BF16)
            return 0

        lax.fori_loop(0, CTX, one_home, 0)

    @pl.when(is_v)
    def _():
        gv = g - KTYPES

        def one_home(c, _):
            r = c * 96
            cg[pl.ds(m16(c * HALF + 48 * gv), 48), :] += rgf[pl.ds(m16(r + 48 * b), 48), :]
            out_ref[c, 96:144, :] = (rgf[pl.ds(m16(r + 48 * (1 - b)), 48), :] * SCALE).astype(BF16)
            return 0

        lax.fori_loop(0, CTX, one_home, 0)

    def columns(c, _):
        out_ref[c, 0:HALF, :] = (cg[pl.ds(m16(c * HALF), HALF), :] * SCALE).astype(BF16)
        out_ref[c, 144:160, :] = pieces
        return 0

    lax.fori_loop(0, CTX, columns, 0)


def loss_kernel(in_ref, loss_ref):
    total = jnp.sum(in_ref[:, 144:160, :].astype(F32), axis=0)
    loss_ref[...] = jnp.sum(total, axis=0, keepdims=True)


def sum_kernel(in_ref, out_ref):
    def at(h, g, b):
        return (h * 8 + g) * 2 + b

    def part(d, lo, n):
        return in_ref[d, lo : lo + n, :].astype(F32)

    for h in range(2):
        lanes = slice(h * WIDTH, (h + 1) * WIDTH)
        for g in range(KTYPES):
            q = part(at(h, g, 0), 96, 32) + part(at(h, g, 1), 96, 32)
            out_ref[0, 16 * g : 16 * g + 16, lanes] = q[:16]
            out_ref[0, HALF + 16 * g : HALF + 16 * g + 16, lanes] = q[16:]
        for b in range(2):
            for g in range(KTYPES):
                own = part(at(h, g, 1 - b), 128, 16)
                for k in range(KTYPES):
                    own += part(at(h, k, b), 16 * g, 16)
                out_ref[1, HALF * b + 16 * g : HALF * b + 16 * g + 16, lanes] = own
            for v in range(2):
                own = part(at(h, KTYPES + v, 1 - b), 96, 48)
                for k in range(2):
                    own += part(at(h, KTYPES + k, b), 48 * v, 48)
                out_ref[2, HALF * b + 48 * v : HALF * b + 48 * v + 48, lanes] = own


def held_arrays(packed):
    return lax.all_to_all(packed, "ctx", 0, 0, tiled=True)


def pack(teacher, student, segment_ids):
    return pl.pallas_call(
        pack_kernel,
        out_shape=jax.ShapeDtypeStruct((CTX, IN_ROWS, WIDTH), BF16),
        in_specs=[pl.BlockSpec(memory_space=pltpu.HBM)] * 3,
        scratch_shapes=[
            pltpu.VMEM((3, HOME, 2 * WIDTH), BF16),
            pltpu.VMEM((3, HOME, 2 * WIDTH), BF16),
            pltpu.VMEM((1, HOME), jnp.int32),
            pltpu.SemaphoreType.DMA((3,)),
        ],
        compiler_params=params(),
        name="pack",
    )(teacher, student, segment_ids.reshape(1, HOME))


LISTS = [pltpu.SMEM((MAXT,), jnp.int32)] * 2


def row_stats(held, name="stats"):
    flat = lambda n: jax.ShapeDtypeStruct((n, WIDTH), BF16)
    return pl.pallas_call(
        stats_kernel,
        out_shape=(
            jax.ShapeDtypeStruct((5, 16, RB), F32),
            flat(PADC), flat(PADC), flat(ROWS), flat(ROWS), flat(PADC), flat(ROWS),
        ),
        scratch_shapes=[pltpu.VMEM((NBLK, 8, RB), F32)] * 5 + LISTS,
        compiler_params=params(),
        name=name,
    )(held)


def turned(cols, name="turn"):
    return pl.pallas_call(
        turn_kernel,
        out_shape=jax.ShapeDtypeStruct((WIDTH, PADC), BF16),
        compiler_params=params(),
        cost_estimate=pl.CostEstimate(flops=10_000_000, bytes_accessed=8_000_000, transcendentals=0),
        name=name,
    )(cols)


def grad_terms(held, flats, keyt, stats, other, name="grads"):
    return pl.pallas_call(
        grads_kernel,
        out_shape=jax.ShapeDtypeStruct((CTX, OUT_ROWS, WIDTH), BF16),
        scratch_shapes=[
            pltpu.VMEM((16, RB), F32),
            pltpu.VMEM((16, RB), F32),
            pltpu.VMEM((PADC, WIDTH), F32),
            pltpu.VMEM((NBLK, WIDTH, RB), F32),
            pltpu.VMEM((ROWS, WIDTH), F32),
        ]
        + LISTS,
        compiler_params=params(),
        name=name,
    )(held, *flats, keyt, stats, other)


def shards(teacher_qkv, student_qkv, segment_ids):
    teacher = jnp.transpose(teacher_qkv, (1, 0, 2))
    student = jnp.transpose(student_qkv, (1, 0, 2))
    held = held_arrays(pack(teacher, student, segment_ids))
    stats, *flats = row_stats(held)
    other = lax.ppermute(stats, "ctx", [(i, i ^ 1) for i in range(CTX)])
    keyt = turned(flats[1])
    terms = grad_terms(held, flats, keyt, stats, other)
    back = lax.all_to_all(terms, "ctx", 0, 0, tiled=True)
    part = pl.pallas_call(
        loss_kernel,
        out_shape=jax.ShapeDtypeStruct((1, WIDTH), F32),
        compiler_params=params(),
        name="loss_part",
    )(back)
    peers = [lax.ppermute(part, "tp", [(i, i ^ k) for i in range(4)]) for k in (1, 2, 3)]
    grad = pl.pallas_call(
        sum_kernel,
        out_shape=jax.ShapeDtypeStruct((3, HOME, 2 * WIDTH), F32),
        compiler_params=params(),
        cost_estimate=pl.CostEstimate(flops=10_000_000, bytes_accessed=8_000_000, transcendentals=0),
        name="home_sum",
    )(back)
    loss = ((part + peers[0]) + (peers[1] + peers[2]))[0, 0] / (CTX * HOME)
    return loss, jnp.transpose(grad, (1, 0, 2))


def solution(mesh):
    return jax.shard_map(
        shards,
        mesh=mesh,
        in_specs=(P("ctx", None, "tp"), P("ctx", None, "tp"), P("ctx")),
        out_specs=(P(), P("ctx", None, "tp")),
        check_vma=False,
    )
```

```python
import math

import jax
import jax.numpy as jnp
from jax import lax
from jax.experimental import pallas as pl
from jax.experimental.pallas import tpu as pltpu
from jax.sharding import PartitionSpec as P

WIDTH = 128
CTX = 32
HOME = 192
HALF = 96
LAST = 5
KTYPES = 6
SCALE = WIDTH**-0.5
LOG2E = math.log2(math.e)
C2 = SCALE * LOG2E
FAR = 2.0**100
NCOLS = CTX * HALF
ROWS = CTX * HALF
RB = 256
CB = 256
NBLK = ROWS // RB
PADC = NCOLS + 256
MAXT = 256
PART = HALF + 48
OUT_ROWS = HALF + 48 + 16
F32 = jnp.float32
BF16 = jnp.bfloat16
NT = (((1,), (1,)), ((), ()))


def params(mib=24, **kw):
    return pltpu.CompilerParams(vmem_limit_bytes=mib * 1024 * 1024, **kw)


def pack_kernel(t_ref, s_ref, seg_ref, out_ref):
    seg = jnp.broadcast_to(seg_ref[...], (16, HOME))
    step = lax.broadcasted_iota(jnp.int32, (16, HOME), 0)
    counts = jnp.sum(jnp.where(seg < step, 1.0, 0.0), axis=1, keepdims=True)
    counts = jnp.broadcast_to(counts, (16, WIDTH)).astype(BF16)
    for d in range(CTX):
        b, g, h = d % 2, (d // 2) % 8, d // 16
        lanes = slice(h * WIDTH, (h + 1) * WIDTH)
        for k, ref in enumerate((t_ref, s_ref)):
            o = k * PART
            part = 1 if g < KTYPES else 2
            out_ref[d, o : o + HALF, :] = ref[part, HALF * b : HALF * b + HALF, lanes]
            o += HALF
            if g < KTYPES:
                out_ref[d, o : o + 16, :] = ref[0, 16 * g : 16 * g + 16, lanes]
                out_ref[d, o + 16 : o + 32, :] = ref[0, HALF + 16 * g : HALF + 16 * g + 16, lanes]
                at = HALF * (1 - b) + 16 * g
                out_ref[d, o + 32 : o + 48, :] = ref[1, at : at + 16, lanes]
            else:
                at = HALF * (1 - b) + 48 * (g - KTYPES)
                out_ref[d, o : o + 48, :] = ref[2, at : at + 48, lanes]
        out_ref[d, 2 * PART :, :] = counts


def place():
    role = lax.axis_index("ctx")
    b = lax.rem(role, 2)
    g = lax.rem(role // 2, 8)
    return b, g, g >= KTYPES


def m16(x):
    return pl.multiple_of(x, 16)


def assemble(in_ref, o, cols, rows, rows_t, b, g, is_v):
    cols[NCOLS:, :] = jnp.zeros((PADC - NCOLS, WIDTH), BF16)

    def columns(c, _):
        cols[pl.ds(m16(c * HALF), HALF), :] = in_ref[c, o : o + HALF, :]
        return 0

    lax.fori_loop(0, CTX, columns, 0, unroll=4)

    @pl.when(jnp.logical_not(is_v))
    def _():
        def one(c, _):
            r = c * 64
            rows[pl.ds(m16(r), 32), :] = in_ref[c, o + 96 : o + 128, :]
            rows[pl.ds(m16(r + 32 + 16 * (1 - b)), 16), :] = in_ref[c, o + 128 : o + 144, :]
            rows[pl.ds(m16(r + 32 + 16 * b), 16), :] = in_ref[c, pl.ds(m16(o + 16 * g), 16), :]
            return 0

        lax.fori_loop(0, CTX, one, 0, unroll=4)

    @pl.when(is_v)
    def _():
        gv = g - KTYPES

        def one(c, _):
            r = c * 96
            rows[pl.ds(m16(r + 48 * (1 - b)), 48), :] = in_ref[c, o + 96 : o + 144, :]
            rows[pl.ds(m16(r + 48 * b), 48), :] = in_ref[c, pl.ds(m16(o + 48 * gv), 48), :]
            return 0

        lax.fori_loop(0, CTX, one, 0, unroll=4)

    for k in range(ROWS // 128):
        at = slice(k * 128, k * 128 + 128)
        rows_t[:, at] = rows[at, :].T


def documents(in_ref, b):
    total = jnp.sum(in_ref[:, 2 * PART :, :].astype(F32), axis=0)
    starts, firsts = [], []
    for d in range(1, LAST + 1):
        t = jnp.max(total[d : d + 1, :]).astype(jnp.int32)
        home = t // HOME
        starts.append(t)
        firsts.append(home * HALF + jnp.clip(t - home * HOME - HALF * b, 0, HALF))
    return starts, firsts


def marks(featc, mask_t, starts, firsts, g, is_v):
    def edges(at, points, rest_lo, rest_hi):
        lo = jnp.full(at.shape, rest_lo, jnp.int32)
        hi = jnp.full(at.shape, rest_hi, jnp.int32)
        for s in range(len(points) - 1):
            lo = jnp.where(at == s, points[s], lo)
            hi = jnp.where(at == s, points[s + 1], hi)
        return lo, hi

    lane = lax.broadcasted_iota(jnp.int32, (1, WIDTH), 1)
    lo, hi = edges(lane, [0, *firsts, NCOLS, PADC], 0, 0)
    ones = (lane >= 16) & (lane < 19)
    lo, hi = jnp.where(ones, 0, lo), jnp.where(ones, PADC, hi)
    at = lax.broadcasted_iota(jnp.int32, (128, WIDTH), 0)

    def column_block(k, _):
        j = at + k * 128
        inside = (j >= lo) & (j < hi)
        featc[pl.ds(pl.multiple_of(k * 128, 128), 128), :] = jnp.where(inside, 1.0, 0.0).astype(BF16)
        return 0

    lax.fori_loop(0, PADC // 128, column_block, 0, unroll=2)
    tokens = CTX * HOME
    entry = lax.broadcasted_iota(jnp.int32, (16, 1), 0)
    lo, hi = edges(entry, [0, *starts, tokens], -1, 2 * tokens)
    lo = jnp.where(entry == LAST + 1, 2 * tokens, lo)
    f = lax.broadcasted_iota(jnp.int32, (1, ROWS), 1)
    i, c = f & 63, f >> 6
    key_token = HOME * c + HALF * ((i >> 4) & 1) + (i & 15) + 16 * g
    c = ((f.astype(F32) + 0.5) * (1.0 / 96.0)).astype(jnp.int32)
    i = f - 96 * c
    value_token = HOME * c + i + jnp.where(i >= 48, 48, 0) + 48 * (g - KTYPES)
    token = jnp.where(is_v, value_token, key_token)
    mask_t[...] = jnp.where((token >= lo) & (token < hi), 0.0, -FAR).astype(BF16)


def list_tiles(tiles, starts, firsts, g, is_v):
    homes = RB // 64

    def value_token(f):
        c = f // 96
        i = f - c * 96
        return HOME * c + jnp.where(i >= 48, i + 48, i) + 48 * (g - KTYPES)

    def block(blk, count):
        first = jnp.where(is_v, value_token(blk * RB), HOME * homes * blk + 16 * g)
        last = jnp.where(
            is_v, value_token(blk * RB + RB - 1), HOME * (homes * blk + homes - 1) + HALF + 16 * g + 15
        )
        c0, c1 = 0, NCOLS
        for t, c in zip(starts, firsts):
            c0 = jnp.where(first >= t, c, c0)
        for t, c in reversed(list(zip(starts, firsts))):
            c1 = jnp.where(last < t, c, c1)
        c0 = lax.shift_left(lax.shift_right_logical(c0, 7), 7)

        def put(c, count):
            tiles[count] = blk * 65536 + c
            return c + CB, count + 1

        _, count = lax.while_loop(lambda s: s[0] < c1, lambda s: put(*s), (c0, count))
        return count

    blocks = jnp.where(is_v, NBLK, CTX * 64 // RB)
    count = lax.fori_loop(0, blocks, block, 1)
    for k in range(5):
        tiles[count + k] = NCOLS
    tiles[0] = count - 1


def spot(tile, tiles):
    code = tiles[tile]
    blk, col = lax.shift_right_logical(code, 16), pl.multiple_of(code & 65535, 128)
    return blk, pl.ds(pl.multiple_of(blk * RB, RB), RB), pl.ds(col, CB)


def stats_kernel(
    in_ref, out_ref, colt, cols, rowt_t, rows_t, featc, mask_t, tiles,
    rowt, rows, top_t, sum_t, top_s, sum_s, at_, as_, bt_, bs_,
):
    b, g, is_v = place()
    starts, firsts = documents(in_ref, b)
    list_tiles(tiles, starts, firsts, g, is_v)
    marks(featc, mask_t, starts, firsts, g, is_v)
    assemble(in_ref, 0, colt, rowt, rowt_t, b, g, is_v)
    assemble(in_ref, PART, cols, rows, rows_t, b, g, is_v)
    for ref in (top_t, top_s):
        ref[...] = jnp.full(ref.shape, -FAR, F32)
    for ref in (sum_t, sum_s):
        ref[...] = jnp.zeros(ref.shape, F32)
    rest = jnp.zeros((WIDTH - 16, RB), BF16)
    count = tiles[0]

    models = ((colt, rowt_t, top_t, sum_t), (cols, rows_t, top_s, sum_s))

    def score(tile, k, buf):
        _, rsl, csl = spot(tile, tiles)
        c_ref, r_ref, _, _ = models[k]
        left = jnp.concatenate([c_ref[csl, :], featc[csl, :]], axis=1)
        right = jnp.concatenate([r_ref[:, rsl], mask_t[:, rsl], rest], axis=0)
        d = jnp.dot(left, right, preferred_element_type=F32)
        buf[...] = d
        return jnp.max(d.reshape(CB // 8, 8, RB), axis=0)

    def gather(tile, k, buf, high):
        blk = spot(tile, tiles)[0]
        _, _, top, total = models[k]
        old = top[blk]
        new = jnp.maximum(old, high)
        acc = total[blk] * jnp.exp2((old - new) * C2)
        for q in range(CB // 16):
            e = jnp.exp2((buf[q * 16 : q * 16 + 16, :].reshape(16 // 8, 8, RB) - new[None]) * C2)
            acc += jnp.sum(e, axis=0)
        total[blk] = acc
        top[blk] = new

    def turn(i, highs):
        ht, hs = highs
        for k in range(4):
            a, b = ((at_, as_), (bt_, bs_)) if k % 2 == 0 else ((bt_, bs_), (at_, as_))
            nt = score(4 * i + k + 2, 0, b[0])
            gather(4 * i + k + 1, 0, a[0], ht)
            ns = score(4 * i + k + 2, 1, b[1])
            gather(4 * i + k + 1, 1, a[1], hs)
            ht, hs = nt, ns
        return ht, hs

    lax.fori_loop(0, (count + 3) // 4, turn, (score(1, 0, at_), score(1, 1, as_)))
    out_ref[...] = jnp.zeros(out_ref.shape, F32)
    for k, (top, total) in enumerate(((top_t, sum_t), (top_s, sum_s))):
        for blk in range(NBLK):
            t = top[blk]
            most = jnp.max(t, axis=0, keepdims=True)
            out_ref[2 * k, blk : blk + 1, :] = most
            out_ref[2 * k + 1, blk : blk + 1, :] = jnp.sum(
                total[blk] * jnp.exp2((t - most) * C2), axis=0, keepdims=True
            )


def turn_kernel(cols, keyt):
    for k in range(PADC // 128):
        at = slice(k * 128, k * 128 + 128)
        keyt[:, at] = cols[at, :].T


def in_three(x):
    high = x.astype(BF16).astype(F32)
    mid = (x - high).astype(BF16).astype(F32)
    low = x - high - mid
    row = lax.broadcasted_iota(jnp.int32, (16, x.shape[1]), 0)
    return jnp.where(row == 0, high, jnp.where(row == 1, mid, jnp.where(row == 2, low, 0.0))).astype(BF16)


def grads_kernel(
    colt, cols, rowt_t, rows_t, keyt, featc, mask_t, tiles, mine, other, out_ref,
    lset, lses, cgt, rgt, cg, rgf, at_, as_, bt_, bs_, ga_, gb_,
):
    b, g, is_v = place()
    count = tiles[0]
    cgt[...] = jnp.zeros(cgt.shape, F32)
    gb_[...] = jnp.zeros(gb_.shape, BF16)
    rgt[...] = jnp.zeros(rgt.shape, F32)

    lses2 = []
    for k in (0, 2):
        top = jnp.maximum(mine[k], other[k])
        total = mine[k + 1] * jnp.exp2((mine[k] - top) * C2) + other[k + 1] * jnp.exp2((other[k] - top) * C2)
        lses2.append(top + jnp.log2(total) * (1.0 / C2))
    for blk in range(NBLK):
        at = slice(blk * RB, blk * RB + RB)
        lset[:, at] = in_three(-lses2[0][blk : blk + 1])
        lses[:, at] = in_three(-lses2[1][blk : blk + 1])
    rest = jnp.zeros((WIDTH - 32, RB), BF16)

    def scores(tile, bufs):
        _, rsl, csl = spot(tile, tiles)
        for c_ref, r_ref, lse, buf in ((colt, rowt_t, lset, bufs[0]), (cols, rows_t, lses, bufs[1])):
            left = jnp.concatenate([c_ref[csl, :], featc[csl, :]], axis=1)
            right = jnp.concatenate([r_ref[:, rsl], mask_t[:, rsl], lse[:, rsl], rest], axis=0)
            buf[...] = jnp.dot(left, right, preferred_element_type=F32)

    def differ(bufs, diff, kl):
        for q in range(0, CB, 16):
            xt, xs = bufs[0][q : q + 16, :], bufs[1][q : q + 16, :]
            pt = jnp.exp2(xt * C2)
            diff[q : q + 16, :] = (jnp.exp2(xs * C2) - pt).astype(BF16)
            kl += jnp.sum((pt * (xt - xs)).reshape(16 // 8, 8, RB), axis=0)
        return kl

    def spread(tile, diff):
        blk, rsl, csl = spot(tile, tiles)
        cgt[:, csl] += lax.dot_general(rows_t[:, rsl], diff[...], NT, preferred_element_type=F32)
        rgt[blk] += jnp.dot(keyt[:, csl], diff[...], preferred_element_type=F32)

    even, odd = (at_, as_), (bt_, bs_)
    turns = (count + 3) // 4

    def turn(i, kl):
        for k in range(4):
            a, b = (even, odd) if k % 2 == 0 else (odd, even)
            da, db = (ga_, gb_) if k % 2 == 0 else (gb_, ga_)
            scores(4 * i + k + 2, b)
            spread(jnp.where(i == 0, count + 1, 4 * i) if k == 0 else 4 * i + k, db)
            kl = differ(a, da, kl)
        return kl

    scores(1, even)
    kl = lax.fori_loop(0, turns, turn, jnp.zeros((8, RB), F32))
    spread(4 * turns, gb_)
    pieces = in_three(jnp.full((1, WIDTH), SCALE, F32) * jnp.sum(kl))

    for k in range(NCOLS // 128):
        cg[k * 128 : k * 128 + 128, :] = cgt[:, k * 128 : k * 128 + 128].T
    for blk in range(NBLK):
        rgf[blk * RB : blk * RB + RB, :] = rgt[blk].T

    @pl.when(jnp.logical_not(is_v))
    def _():
        def one_home(c, _):
            r = c * 64
            cg[pl.ds(m16(c * HALF + 16 * g), 16), :] += rgf[pl.ds(m16(r + 32 + 16 * b), 16), :]
            out_ref[c, 96:128, :] = (rgf[pl.ds(m16(r), 32), :] * SCALE).astype(BF16)
            out_ref[c, 128:144, :] = (rgf[pl.ds(m16(r + 32 + 16 * (1 - b)), 16), :] * SCALE).astype(BF16)
            return 0

        lax.fori_loop(0, CTX, one_home, 0)

    @pl.when(is_v)
    def _():
        gv = g - KTYPES

        def one_home(c, _):
            r = c * 96
            cg[pl.ds(m16(c * HALF + 48 * gv), 48), :] += rgf[pl.ds(m16(r + 48 * b), 48), :]
            out_ref[c, 96:144, :] = (rgf[pl.ds(m16(r + 48 * (1 - b)), 48), :] * SCALE).astype(BF16)
            return 0

        lax.fori_loop(0, CTX, one_home, 0)

    def columns(c, _):
        out_ref[c, 0:HALF, :] = (cg[pl.ds(m16(c * HALF), HALF), :] * SCALE).astype(BF16)
        out_ref[c, 144:160, :] = pieces
        return 0

    lax.fori_loop(0, CTX, columns, 0)


def loss_kernel(in_ref, loss_ref):
    total = jnp.sum(in_ref[:, 144:160, :].astype(F32), axis=0)
    loss_ref[...] = jnp.sum(total, axis=0, keepdims=True)


def sum_kernel(in_ref, out_ref):
    def at(h, g, b):
        return (h * 8 + g) * 2 + b

    def part(d, lo, n):
        return in_ref[d, lo : lo + n, :].astype(F32)

    for h in range(2):
        lanes = slice(h * WIDTH, (h + 1) * WIDTH)
        for g in range(KTYPES):
            q = part(at(h, g, 0), 96, 32) + part(at(h, g, 1), 96, 32)
            out_ref[0, 16 * g : 16 * g + 16, lanes] = q[:16]
            out_ref[0, HALF + 16 * g : HALF + 16 * g + 16, lanes] = q[16:]
        for b in range(2):
            for g in range(KTYPES):
                own = part(at(h, g, 1 - b), 128, 16)
                for k in range(KTYPES):
                    own += part(at(h, k, b), 16 * g, 16)
                out_ref[1, HALF * b + 16 * g : HALF * b + 16 * g + 16, lanes] = own
            for v in range(2):
                own = part(at(h, KTYPES + v, 1 - b), 96, 48)
                for k in range(2):
                    own += part(at(h, KTYPES + k, b), 48 * v, 48)
                out_ref[2, HALF * b + 48 * v : HALF * b + 48 * v + 48, lanes] = own


def bf16(*shape):
    return jax.ShapeDtypeStruct(shape, BF16)


def pack(teacher, student, segment_ids):
    return pl.pallas_call(
        pack_kernel,
        out_shape=bf16(CTX, 2 * PART + 16, WIDTH),
        compiler_params=params(),
        name="pack",
    )(teacher, student, segment_ids.reshape(1, HOME))


TILE = pltpu.VMEM((CB, RB), F32)


def row_stats(held, name="stats"):
    in_vmem, in_smem = pl.BlockSpec(memory_space=pltpu.VMEM), pl.BlockSpec(memory_space=pltpu.SMEM)
    return pl.pallas_call(
        stats_kernel,
        out_shape=[
            jax.ShapeDtypeStruct((4, 16, RB), F32),
            bf16(PADC, WIDTH), bf16(PADC, WIDTH), bf16(WIDTH, ROWS), bf16(WIDTH, ROWS), bf16(PADC, WIDTH), bf16(16, ROWS),
            jax.ShapeDtypeStruct((MAXT,), jnp.int32),
        ],
        out_specs=[in_vmem] * 7 + [in_smem],
        scratch_shapes=[pltpu.VMEM((ROWS, WIDTH), BF16)] * 2 + [pltpu.VMEM((NBLK, 8, RB), F32)] * 4 + [TILE] * 4,
        compiler_params=params(),
        name=name,
    )(held)


def turned(cols, name="turn"):
    return pl.pallas_call(
        turn_kernel,
        out_shape=bf16(WIDTH, PADC),
        compiler_params=params(),
        cost_estimate=pl.CostEstimate(flops=10_000_000, bytes_accessed=8_000_000, transcendentals=0),
        name=name,
    )(cols)


def grad_terms(found, keyt, other, name="grads"):
    stats, colt, cols, rowt_t, rows_t, featc, mask_t, tiles = found
    in_vmem, in_smem = pl.BlockSpec(memory_space=pltpu.VMEM), pl.BlockSpec(memory_space=pltpu.SMEM)
    return pl.pallas_call(
        grads_kernel,
        out_shape=bf16(CTX, OUT_ROWS, WIDTH),
        in_specs=[in_vmem] * 7 + [in_smem] + [in_vmem] * 2,
        scratch_shapes=[
            pltpu.VMEM((16, ROWS), BF16),
            pltpu.VMEM((16, ROWS), BF16),
            pltpu.VMEM((WIDTH, PADC), F32),
            pltpu.VMEM((NBLK, WIDTH, RB), F32),
            pltpu.VMEM((NCOLS, WIDTH), F32),
            pltpu.VMEM((ROWS, WIDTH), F32),
        ]
        + [TILE] * 4
        + [pltpu.VMEM((CB, RB), BF16)] * 2,
        compiler_params=params(),
        name=name,
    )(colt, cols, rowt_t, rows_t, keyt, featc, mask_t, tiles, stats, other)


def swap(stats):
    return lax.ppermute(stats, "ctx", [(i, i ^ 1) for i in range(CTX)])


def shards(teacher_qkv, student_qkv, segment_ids):
    teacher = jnp.transpose(teacher_qkv, (1, 0, 2))
    student = jnp.transpose(student_qkv, (1, 0, 2))
    held = lax.all_to_all(pack(teacher, student, segment_ids), "ctx", 0, 0, tiled=True)
    found = row_stats(held)
    other = swap(found[0])
    terms = grad_terms(found, turned(found[2]), other)
    back = lax.all_to_all(terms, "ctx", 0, 0, tiled=True)
    part = pl.pallas_call(
        loss_kernel,
        out_shape=jax.ShapeDtypeStruct((1, WIDTH), F32),
        compiler_params=params(),
        name="loss_part",
    )(back)
    peers = [lax.ppermute(part, "tp", [(i, i ^ k) for i in range(4)]) for k in (1, 2, 3)]
    grad = pl.pallas_call(
        sum_kernel,
        out_shape=jax.ShapeDtypeStruct((3, HOME, 2 * WIDTH), F32),
        compiler_params=params(),
        cost_estimate=pl.CostEstimate(flops=10_000_000, bytes_accessed=8_000_000, transcendentals=0),
        name="home_sum",
    )(back)
    loss = ((part + peers[0]) + (peers[1] + peers[2]))[0, 0] / (CTX * HOME)
    return loss, jnp.transpose(grad, (1, 0, 2))


def solution(mesh):
    return jax.shard_map(
        shards,
        mesh=mesh,
        in_specs=(P("ctx", None, "tp"), P("ctx", None, "tp"), P("ctx")),
        out_specs=(P(), P("ctx", None, "tp")),
        check_vma=False,
    )
```

```python
import math

import jax
import jax.numpy as jnp
from jax import lax
from jax.experimental import pallas as pl
from jax.experimental.pallas import tpu as pltpu
from jax.sharding import PartitionSpec as P

WIDTH = 128
CTX = 32
HOME = 192
HALF = 96
LAST = 5
KTYPES = 6
SCALE = WIDTH**-0.5
LOG2E = math.log2(math.e)
C2 = SCALE * LOG2E
FAR = 2.0**100
NCOLS = CTX * HALF
ROWS = CTX * HALF
RB = 256
CB = 256
NBLK = ROWS // RB
PADC = NCOLS + 256
UNROLL = 4
MOST_TURNS = NCOLS // CB + 1
MAXT = 256
PART = HALF + 48
OUT_ROWS = HALF + 48 + 16
F32 = jnp.float32
BF16 = jnp.bfloat16
NT = (((1,), (1,)), ((), ()))


def params(mib=24, **kw):
    return pltpu.CompilerParams(vmem_limit_bytes=mib * 1024 * 1024, **kw)


def pack_kernel(t_ref, s_ref, seg_ref, out_ref):
    seg = jnp.broadcast_to(seg_ref[...], (16, HOME))
    step = lax.broadcasted_iota(jnp.int32, (16, HOME), 0)
    counts = jnp.sum(jnp.where(seg < step, 1.0, 0.0), axis=1, keepdims=True)
    counts = jnp.broadcast_to(counts, (16, WIDTH)).astype(BF16)
    for d in range(CTX):
        b, g, h = d % 2, (d // 2) % 8, d // 16
        lanes = slice(h * WIDTH, (h + 1) * WIDTH)
        for k, ref in enumerate((t_ref, s_ref)):
            o = k * PART
            part = 1 if g < KTYPES else 2
            out_ref[d, o : o + HALF, :] = ref[part, HALF * b : HALF * b + HALF, lanes]
            o += HALF
            if g < KTYPES:
                out_ref[d, o : o + 16, :] = ref[0, 16 * g : 16 * g + 16, lanes]
                out_ref[d, o + 16 : o + 32, :] = ref[0, HALF + 16 * g : HALF + 16 * g + 16, lanes]
                at = HALF * (1 - b) + 16 * g
                out_ref[d, o + 32 : o + 48, :] = ref[1, at : at + 16, lanes]
            else:
                at = HALF * (1 - b) + 48 * (g - KTYPES)
                out_ref[d, o : o + 48, :] = ref[2, at : at + 48, lanes]
        out_ref[d, 2 * PART :, :] = counts


def place():
    role = lax.axis_index("ctx")
    b = lax.rem(role, 2)
    g = lax.rem(role // 2, 8)
    return b, g, g >= KTYPES


def m16(x):
    return pl.multiple_of(x, 16)


def assemble(in_ref, o, cols, rows, rows_t, b, g, is_v):
    cols[NCOLS:, :] = jnp.zeros((PADC - NCOLS, WIDTH), BF16)

    def columns(c, _):
        cols[pl.ds(m16(c * HALF), HALF), :] = in_ref[c, o : o + HALF, :]
        return 0

    lax.fori_loop(0, CTX, columns, 0, unroll=4)

    @pl.when(jnp.logical_not(is_v))
    def _():
        def one(c, _):
            r = c * 64
            rows[pl.ds(m16(r), 32), :] = in_ref[c, o + 96 : o + 128, :]
            rows[pl.ds(m16(r + 32 + 16 * (1 - b)), 16), :] = in_ref[c, o + 128 : o + 144, :]
            rows[pl.ds(m16(r + 32 + 16 * b), 16), :] = in_ref[c, pl.ds(m16(o + 16 * g), 16), :]
            return 0

        lax.fori_loop(0, CTX, one, 0, unroll=4)

    @pl.when(is_v)
    def _():
        gv = g - KTYPES

        def one(c, _):
            r = c * 96
            rows[pl.ds(m16(r + 48 * (1 - b)), 48), :] = in_ref[c, o + 96 : o + 144, :]
            rows[pl.ds(m16(r + 48 * b), 48), :] = in_ref[c, pl.ds(m16(o + 48 * gv), 48), :]
            return 0

        lax.fori_loop(0, CTX, one, 0, unroll=4)

    for k in range(ROWS // 128):
        at = slice(k * 128, k * 128 + 128)
        rows_t[:, at] = rows[at, :].T


def documents(in_ref, b):
    total = jnp.sum(in_ref[:, 2 * PART :, :].astype(F32), axis=0)
    starts, firsts = [], []
    for d in range(1, LAST + 1):
        t = jnp.max(total[d : d + 1, :]).astype(jnp.int32)
        home = t // HOME
        starts.append(t)
        firsts.append(home * HALF + jnp.clip(t - home * HOME - HALF * b, 0, HALF))
    return starts, firsts


def marks(featc, mask_t, starts, firsts, g, is_v):
    def edges(at, points, rest_lo, rest_hi):
        lo = jnp.full(at.shape, rest_lo, jnp.int32)
        hi = jnp.full(at.shape, rest_hi, jnp.int32)
        for s in range(len(points) - 1):
            lo = jnp.where(at == s, points[s], lo)
            hi = jnp.where(at == s, points[s + 1], hi)
        return lo, hi

    lane = lax.broadcasted_iota(jnp.int32, (1, WIDTH), 1)
    lo, hi = edges(lane, [0, *firsts, NCOLS, PADC], 0, 0)
    ones = (lane >= 16) & (lane < 19)
    lo, hi = jnp.where(ones, 0, lo), jnp.where(ones, PADC, hi)
    at = lax.broadcasted_iota(jnp.int32, (128, WIDTH), 0)

    def column_block(k, _):
        j = at + k * 128
        inside = (j >= lo) & (j < hi)
        featc[pl.ds(pl.multiple_of(k * 128, 128), 128), :] = jnp.where(inside, 1.0, 0.0).astype(BF16)
        return 0

    lax.fori_loop(0, PADC // 128, column_block, 0, unroll=2)
    tokens = CTX * HOME
    entry = lax.broadcasted_iota(jnp.int32, (16, 1), 0)
    lo, hi = edges(entry, [0, *starts, tokens], -1, 2 * tokens)
    lo = jnp.where(entry == LAST + 1, 2 * tokens, lo)
    f = lax.broadcasted_iota(jnp.int32, (1, ROWS), 1)
    i, c = f & 63, f >> 6
    key_token = HOME * c + HALF * ((i >> 4) & 1) + (i & 15) + 16 * g
    c = ((f.astype(F32) + 0.5) * (1.0 / 96.0)).astype(jnp.int32)
    i = f - 96 * c
    value_token = HOME * c + i + jnp.where(i >= 48, 48, 0) + 48 * (g - KTYPES)
    token = jnp.where(is_v, value_token, key_token)
    mask_t[...] = jnp.where((token >= lo) & (token < hi), 0.0, -FAR).astype(BF16)


def list_tiles(tiles, starts, firsts, g, is_v):
    homes = RB // 64

    def value_token(f):
        c = f // 96
        i = f - c * 96
        return HOME * c + jnp.where(i >= 48, i + 48, i) + 48 * (g - KTYPES)

    def block(blk, count):
        first = jnp.where(is_v, value_token(blk * RB), HOME * homes * blk + 16 * g)
        last = jnp.where(
            is_v, value_token(blk * RB + RB - 1), HOME * (homes * blk + homes - 1) + HALF + 16 * g + 15
        )
        c0, c1 = 0, NCOLS
        for t, c in zip(starts, firsts):
            c0 = jnp.where(first >= t, c, c0)
        for t, c in reversed(list(zip(starts, firsts))):
            c1 = jnp.where(last < t, c, c1)
        c0 = lax.shift_left(lax.shift_right_logical(c0, 4), 4)
        for k in range(MOST_TURNS):
            tiles[count + k] = blk * 65536 + c0 + k * CB
        return count + lax.div(c1 - c0 + CB - 1, CB)

    blocks = jnp.where(is_v, NBLK, CTX * 64 // RB)
    count = jnp.int32(1)
    for blk in range(NBLK):
        count = jnp.where(blk < blocks, block(blk, count), count)
    for k in range(UNROLL + 1):
        tiles[count + k] = NCOLS
    tiles[0] = count - 1


def spot(tile, tiles):
    code = tiles[tile]
    blk, col = lax.shift_right_logical(code, 16), m16(code & 65535)
    return blk, pl.ds(pl.multiple_of(blk * RB, RB), RB), pl.ds(col, CB)


def stats_kernel(
    in_ref, out_ref, colt, cols, rowt_t, rows_t, featc, mask_t, tiles,
    rowt, rows, top_t, sum_t, top_s, sum_s, at_, as_, bt_, bs_,
):
    b, g, is_v = place()
    starts, firsts = documents(in_ref, b)
    list_tiles(tiles, starts, firsts, g, is_v)
    marks(featc, mask_t, starts, firsts, g, is_v)
    assemble(in_ref, 0, colt, rowt, rowt_t, b, g, is_v)
    assemble(in_ref, PART, cols, rows, rows_t, b, g, is_v)
    for ref in (top_t, top_s):
        ref[...] = jnp.full(ref.shape, -FAR, F32)
    for ref in (sum_t, sum_s):
        ref[...] = jnp.zeros(ref.shape, F32)
    rest = jnp.zeros((WIDTH - 16, RB), BF16)
    count = tiles[0]

    models = ((colt, rowt_t, top_t, sum_t), (cols, rows_t, top_s, sum_s))

    def score(tile, k, buf):
        _, rsl, csl = spot(tile, tiles)
        c_ref, r_ref, _, _ = models[k]
        left = jnp.concatenate([c_ref[csl, :], featc[csl, :]], axis=1)
        right = jnp.concatenate([r_ref[:, rsl], mask_t[:, rsl], rest], axis=0)
        d = jnp.dot(left, right, preferred_element_type=F32)
        buf[...] = d
        return jnp.max(d.reshape(CB // 8, 8, RB), axis=0)

    def gather(tile, k, buf, high):
        blk = spot(tile, tiles)[0]
        _, _, top, total = models[k]
        old = top[blk]
        new = jnp.maximum(old, high)
        acc = total[blk] * jnp.exp2((old - new) * C2)
        for q in range(CB // 16):
            e = jnp.exp2((buf[q * 16 : q * 16 + 16, :].reshape(16 // 8, 8, RB) - new[None]) * C2)
            acc += jnp.sum(e, axis=0)
        total[blk] = acc
        top[blk] = new

    def turn(i, highs):
        ht, hs = highs
        for k in range(UNROLL):
            a, b = ((at_, as_), (bt_, bs_)) if k % 2 == 0 else ((bt_, bs_), (at_, as_))
            nt = score(UNROLL * i + k + 2, 0, b[0])
            gather(UNROLL * i + k + 1, 0, a[0], ht)
            ns = score(UNROLL * i + k + 2, 1, b[1])
            gather(UNROLL * i + k + 1, 1, a[1], hs)
            ht, hs = nt, ns
        return ht, hs

    lax.fori_loop(0, (count + UNROLL - 1) // UNROLL, turn, (score(1, 0, at_), score(1, 1, as_)))
    out_ref[...] = jnp.zeros(out_ref.shape, F32)
    for k, (top, total) in enumerate(((top_t, sum_t), (top_s, sum_s))):
        for blk in range(NBLK):
            t = top[blk]
            most = jnp.max(t, axis=0, keepdims=True)
            out_ref[2 * k, blk : blk + 1, :] = most
            out_ref[2 * k + 1, blk : blk + 1, :] = jnp.sum(
                total[blk] * jnp.exp2((t - most) * C2), axis=0, keepdims=True
            )


def in_three(x):
    high = x.astype(BF16).astype(F32)
    mid = (x - high).astype(BF16).astype(F32)
    low = x - high - mid
    row = lax.broadcasted_iota(jnp.int32, (16, x.shape[1]), 0)
    return jnp.where(row == 0, high, jnp.where(row == 1, mid, jnp.where(row == 2, low, 0.0))).astype(BF16)


def grads_kernel(
    colt, cols, rowt_t, rows_t, featc, mask_t, tiles, mine, other, out_ref,
    lset, lses, rgt, cg, rgf, at_, as_, bt_, bs_, ga_, gb_,
):
    b, g, is_v = place()
    count = tiles[0]
    cg[...] = jnp.zeros(cg.shape, F32)
    gb_[...] = jnp.zeros(gb_.shape, BF16)
    rgt[...] = jnp.zeros(rgt.shape, F32)

    lses2 = []
    for k in (0, 2):
        top = jnp.maximum(mine[k], other[k])
        total = mine[k + 1] * jnp.exp2((mine[k] - top) * C2) + other[k + 1] * jnp.exp2((other[k] - top) * C2)
        lses2.append(top + jnp.log2(total) * (1.0 / C2))
    for blk in range(NBLK):
        at = slice(blk * RB, blk * RB + RB)
        lset[:, at] = in_three(-lses2[0][blk : blk + 1])
        lses[:, at] = in_three(-lses2[1][blk : blk + 1])
    rest = jnp.zeros((WIDTH - 32, RB), BF16)

    def scores(tile, bufs):
        _, rsl, csl = spot(tile, tiles)
        for c_ref, r_ref, lse, buf in ((colt, rowt_t, lset, bufs[0]), (cols, rows_t, lses, bufs[1])):
            left = jnp.concatenate([c_ref[csl, :], featc[csl, :]], axis=1)
            right = jnp.concatenate([r_ref[:, rsl], mask_t[:, rsl], lse[:, rsl], rest], axis=0)
            buf[...] = jnp.dot(left, right, preferred_element_type=F32)

    def differ(bufs, diff, kl):
        for q in range(0, CB, 16):
            xt, xs = bufs[0][q : q + 16, :], bufs[1][q : q + 16, :]
            pt = jnp.exp2(xt * C2)
            diff[q : q + 16, :] = (jnp.exp2(xs * C2) - pt).astype(BF16)
            kl += jnp.sum((pt * (xt - xs)).reshape(16 // 8, 8, RB), axis=0)
        return kl

    def spread(tile, diff):
        blk, rsl, csl = spot(tile, tiles)
        cg[csl, :] += lax.dot_general(diff[...], rows_t[:, rsl], NT, preferred_element_type=F32)
        rgt[blk] += lax.dot_general(cols[csl, :], diff[...], (((0,), (0,)), ((), ())), preferred_element_type=F32)

    even, odd = (at_, as_), (bt_, bs_)
    turns = (count + UNROLL - 1) // UNROLL

    def turn(i, kl):
        for k in range(UNROLL):
            a, b = (even, odd) if k % 2 == 0 else (odd, even)
            da, db = (ga_, gb_) if k % 2 == 0 else (gb_, ga_)
            scores(UNROLL * i + k + 2, b)
            spread(jnp.where(i == 0, count + 1, UNROLL * i) if k == 0 else UNROLL * i + k, db)
            kl = differ(a, da, kl)
        return kl

    scores(1, even)
    kl = lax.fori_loop(0, turns, turn, jnp.zeros((8, RB), F32))
    spread(UNROLL * turns, gb_)
    pieces = in_three(jnp.full((1, WIDTH), SCALE, F32) * jnp.sum(kl))

    for blk in range(NBLK):
        rgf[blk * RB : blk * RB + RB, :] = rgt[blk].T

    @pl.when(jnp.logical_not(is_v))
    def _():
        def one_home(c, _):
            r = c * 64
            cg[pl.ds(m16(c * HALF + 16 * g), 16), :] += rgf[pl.ds(m16(r + 32 + 16 * b), 16), :]
            out_ref[c, 96:128, :] = (rgf[pl.ds(m16(r), 32), :] * SCALE).astype(BF16)
            out_ref[c, 128:144, :] = (rgf[pl.ds(m16(r + 32 + 16 * (1 - b)), 16), :] * SCALE).astype(BF16)
            return 0

        lax.fori_loop(0, CTX, one_home, 0)

    @pl.when(is_v)
    def _():
        gv = g - KTYPES

        def one_home(c, _):
            r = c * 96
            cg[pl.ds(m16(c * HALF + 48 * gv), 48), :] += rgf[pl.ds(m16(r + 48 * b), 48), :]
            out_ref[c, 96:144, :] = (rgf[pl.ds(m16(r + 48 * (1 - b)), 48), :] * SCALE).astype(BF16)
            return 0

        lax.fori_loop(0, CTX, one_home, 0)

    def columns(c, _):
        out_ref[c, 0:HALF, :] = (cg[pl.ds(m16(c * HALF), HALF), :] * SCALE).astype(BF16)
        out_ref[c, 144:160, :] = pieces
        return 0

    lax.fori_loop(0, CTX, columns, 0)


def loss_kernel(in_ref, loss_ref):
    total = jnp.sum(in_ref[:, 144:160, :].astype(F32), axis=0)
    loss_ref[...] = jnp.sum(total, axis=0, keepdims=True)


def sum_kernel(in_ref, out_ref):
    def at(h, g, b):
        return (h * 8 + g) * 2 + b

    def part(d, lo, n):
        return in_ref[d, lo : lo + n, :].astype(F32)

    for h in range(2):
        lanes = slice(h * WIDTH, (h + 1) * WIDTH)
        for g in range(KTYPES):
            q = part(at(h, g, 0), 96, 32) + part(at(h, g, 1), 96, 32)
            out_ref[0, 16 * g : 16 * g + 16, lanes] = q[:16]
            out_ref[0, HALF + 16 * g : HALF + 16 * g + 16, lanes] = q[16:]
        for b in range(2):
            for g in range(KTYPES):
                own = part(at(h, g, 1 - b), 128, 16)
                for k in range(KTYPES):
                    own += part(at(h, k, b), 16 * g, 16)
                out_ref[1, HALF * b + 16 * g : HALF * b + 16 * g + 16, lanes] = own
            for v in range(2):
                own = part(at(h, KTYPES + v, 1 - b), 96, 48)
                for k in range(2):
                    own += part(at(h, KTYPES + k, b), 48 * v, 48)
                out_ref[2, HALF * b + 48 * v : HALF * b + 48 * v + 48, lanes] = own


def bf16(*shape):
    return jax.ShapeDtypeStruct(shape, BF16)


def pack(teacher, student, segment_ids):
    return pl.pallas_call(
        pack_kernel,
        out_shape=bf16(CTX, 2 * PART + 16, WIDTH),
        compiler_params=params(),
        name="pack",
    )(teacher, student, segment_ids.reshape(1, HOME))


TILE = pltpu.VMEM((CB, RB), F32)


def row_stats(held, name="stats"):
    in_vmem, in_smem = pl.BlockSpec(memory_space=pltpu.VMEM), pl.BlockSpec(memory_space=pltpu.SMEM)
    return pl.pallas_call(
        stats_kernel,
        out_shape=[
            jax.ShapeDtypeStruct((4, 16, RB), F32),
            bf16(PADC, WIDTH), bf16(PADC, WIDTH), bf16(WIDTH, ROWS), bf16(WIDTH, ROWS), bf16(PADC, WIDTH), bf16(16, ROWS),
            jax.ShapeDtypeStruct((MAXT,), jnp.int32),
        ],
        out_specs=[in_vmem] * 7 + [in_smem],
        scratch_shapes=[pltpu.VMEM((ROWS, WIDTH), BF16)] * 2 + [pltpu.VMEM((NBLK, 8, RB), F32)] * 4 + [TILE] * 4,
        compiler_params=params(),
        name=name,
    )(held)


def grad_terms(found, other, name="grads"):
    stats, colt, cols, rowt_t, rows_t, featc, mask_t, tiles = found
    in_vmem, in_smem = pl.BlockSpec(memory_space=pltpu.VMEM), pl.BlockSpec(memory_space=pltpu.SMEM)
    return pl.pallas_call(
        grads_kernel,
        out_shape=bf16(CTX, OUT_ROWS, WIDTH),
        in_specs=[in_vmem] * 6 + [in_smem] + [in_vmem] * 2,
        scratch_shapes=[
            pltpu.VMEM((16, ROWS), BF16),
            pltpu.VMEM((16, ROWS), BF16),
            pltpu.VMEM((NBLK, WIDTH, RB), F32),
            pltpu.VMEM((PADC, WIDTH), F32),
            pltpu.VMEM((ROWS, WIDTH), F32),
        ]
        + [TILE] * 4
        + [pltpu.VMEM((CB, RB), BF16)] * 2,
        compiler_params=params(),
        name=name,
    )(colt, cols, rowt_t, rows_t, featc, mask_t, tiles, stats, other)


def swap(stats):
    return lax.ppermute(stats, "ctx", [(i, i ^ 1) for i in range(CTX)])


def shards(teacher_qkv, student_qkv, segment_ids):
    teacher = jnp.transpose(teacher_qkv, (1, 0, 2))
    student = jnp.transpose(student_qkv, (1, 0, 2))
    held = lax.all_to_all(pack(teacher, student, segment_ids), "ctx", 0, 0, tiled=True)
    found = row_stats(held)
    other = swap(found[0])
    terms = grad_terms(found, other)
    back = lax.all_to_all(terms, "ctx", 0, 0, tiled=True)
    part = pl.pallas_call(
        loss_kernel,
        out_shape=jax.ShapeDtypeStruct((1, WIDTH), F32),
        compiler_params=params(),
        name="loss_part",
    )(back)
    peers = [lax.ppermute(part, "tp", [(i, i ^ k) for i in range(4)]) for k in (1, 2, 3)]
    grad = pl.pallas_call(
        sum_kernel,
        out_shape=jax.ShapeDtypeStruct((3, HOME, 2 * WIDTH), F32),
        compiler_params=params(),
        cost_estimate=pl.CostEstimate(flops=10_000_000, bytes_accessed=8_000_000, transcendentals=0),
        name="home_sum",
    )(back)
    loss = ((part + peers[0]) + (peers[1] + peers[2]))[0, 0] / (CTX * HOME)
    return loss, jnp.transpose(grad, (1, 0, 2))


def solution(mesh):
    return jax.shard_map(
        shards,
        mesh=mesh,
        in_specs=(P("ctx", None, "tp"), P("ctx", None, "tp"), P("ctx")),
        out_specs=(P(), P("ctx", None, "tp")),
        check_vma=False,
    )
```

```python
import math

import jax
import jax.numpy as jnp
from jax import lax
from jax.experimental import pallas as pl
from jax.experimental.pallas import tpu as pltpu
from jax.sharding import PartitionSpec as P

WIDTH = 128
CTX = 32
HOME = 192
HALF = 96
LAST = 5
KTYPES = 6
SCALE = WIDTH**-0.5
LOG2E = math.log2(math.e)
C2 = SCALE * LOG2E
FAR = 2.0**100
NCOLS = CTX * HALF
ROWS = CTX * HALF
RB = 256
CB = 256
NBLK = ROWS // RB
PADC = NCOLS + 256
UNROLL = 4
MOST_TURNS = NCOLS // CB + 1
MAXT = 256
PART = HALF + 48
EXTRA = 8
OUT_ROWS = HALF + 48 + EXTRA
F32 = jnp.float32
BF16 = jnp.bfloat16
NT = (((1,), (1,)), ((), ()))


def params(mib=24, **kw):
    return pltpu.CompilerParams(vmem_limit_bytes=mib * 1024 * 1024, **kw)


def pack_kernel(t_ref, s_ref, seg_ref, out_ref):
    seg = jnp.broadcast_to(seg_ref[...], (EXTRA, HOME))
    step = lax.broadcasted_iota(jnp.int32, (EXTRA, HOME), 0)
    counts = jnp.sum(jnp.where(seg < step, 1.0, 0.0), axis=1, keepdims=True)
    counts = jnp.broadcast_to(counts, (EXTRA, WIDTH)).astype(BF16)
    for d in range(CTX):
        b, g, h = d % 2, (d // 2) % 8, d // 16
        lanes = slice(h * WIDTH, (h + 1) * WIDTH)
        for k, ref in enumerate((t_ref, s_ref)):
            o = k * PART
            part = 1 if g < KTYPES else 2
            out_ref[d, o : o + HALF, :] = ref[part, HALF * b : HALF * b + HALF, lanes]
            o += HALF
            if g < KTYPES:
                out_ref[d, o : o + 16, :] = ref[0, 16 * g : 16 * g + 16, lanes]
                out_ref[d, o + 16 : o + 32, :] = ref[0, HALF + 16 * g : HALF + 16 * g + 16, lanes]
                at = HALF * (1 - b) + 16 * g
                out_ref[d, o + 32 : o + 48, :] = ref[1, at : at + 16, lanes]
            else:
                at = HALF * (1 - b) + 48 * (g - KTYPES)
                out_ref[d, o : o + 48, :] = ref[2, at : at + 48, lanes]
        out_ref[d, 2 * PART :, :] = counts


def place():
    role = lax.axis_index("ctx")
    b = lax.rem(role, 2)
    g = lax.rem(role // 2, 8)
    return b, g, g >= KTYPES


def m16(x):
    return pl.multiple_of(x, 16)


def assemble(in_ref, o, cols, rows, rows_t, b, g, is_v):
    cols[NCOLS:, :] = jnp.zeros((PADC - NCOLS, WIDTH), BF16)

    def columns(c, _):
        cols[pl.ds(m16(c * HALF), HALF), :] = in_ref[c, o : o + HALF, :]
        return 0

    lax.fori_loop(0, CTX, columns, 0, unroll=4)

    @pl.when(jnp.logical_not(is_v))
    def _():
        def one(c, _):
            r = c * 64
            rows[pl.ds(m16(r), 32), :] = in_ref[c, o + 96 : o + 128, :]
            rows[pl.ds(m16(r + 32 + 16 * (1 - b)), 16), :] = in_ref[c, o + 128 : o + 144, :]
            rows[pl.ds(m16(r + 32 + 16 * b), 16), :] = in_ref[c, pl.ds(m16(o + 16 * g), 16), :]
            return 0

        lax.fori_loop(0, CTX, one, 0, unroll=4)

    @pl.when(is_v)
    def _():
        gv = g - KTYPES

        def one(c, _):
            r = c * 96
            rows[pl.ds(m16(r + 48 * (1 - b)), 48), :] = in_ref[c, o + 96 : o + 144, :]
            rows[pl.ds(m16(r + 48 * b), 48), :] = in_ref[c, pl.ds(m16(o + 48 * gv), 48), :]
            return 0

        lax.fori_loop(0, CTX, one, 0, unroll=4)

    for k in range(ROWS // 128):
        at = slice(k * 128, k * 128 + 128)
        rows_t[:, at] = rows[at, :].T


def documents(in_ref, b):
    total = jnp.sum(in_ref[:, 2 * PART :, :].astype(F32), axis=0)
    starts, firsts = [], []
    for d in range(1, LAST + 1):
        t = jnp.max(total[d : d + 1, :]).astype(jnp.int32)
        home = t // HOME
        starts.append(t)
        firsts.append(home * HALF + jnp.clip(t - home * HOME - HALF * b, 0, HALF))
    return starts, firsts


def marks(featc, mask_t, starts, firsts, g, is_v):
    def edges(at, points, rest_lo, rest_hi):
        lo = jnp.full(at.shape, rest_lo, jnp.int32)
        hi = jnp.full(at.shape, rest_hi, jnp.int32)
        for s in range(len(points) - 1):
            lo = jnp.where(at == s, points[s], lo)
            hi = jnp.where(at == s, points[s + 1], hi)
        return lo, hi

    lane = lax.broadcasted_iota(jnp.int32, (1, WIDTH), 1)
    lo, hi = edges(lane, [0, *firsts, NCOLS, PADC], 0, 0)
    ones = (lane >= 16) & (lane < 19)
    lo, hi = jnp.where(ones, 0, lo), jnp.where(ones, PADC, hi)
    at = lax.broadcasted_iota(jnp.int32, (128, WIDTH), 0)

    def column_block(k, _):
        j = at + k * 128
        inside = (j >= lo) & (j < hi)
        featc[pl.ds(pl.multiple_of(k * 128, 128), 128), :] = jnp.where(inside, 1.0, 0.0).astype(BF16)
        return 0

    lax.fori_loop(0, PADC // 128, column_block, 0, unroll=True)
    tokens = CTX * HOME
    entry = lax.broadcasted_iota(jnp.int32, (16, 1), 0)
    lo, hi = edges(entry, [0, *starts, tokens], -1, 2 * tokens)
    lo = jnp.where(entry == LAST + 1, 2 * tokens, lo)
    f = lax.broadcasted_iota(jnp.int32, (1, ROWS), 1)
    i, c = f & 63, f >> 6
    key_token = HOME * c + HALF * ((i >> 4) & 1) + (i & 15) + 16 * g
    c = ((f.astype(F32) + 0.5) * (1.0 / 96.0)).astype(jnp.int32)
    i = f - 96 * c
    value_token = HOME * c + i + jnp.where(i >= 48, 48, 0) + 48 * (g - KTYPES)
    token = jnp.where(is_v, value_token, key_token)
    mask_t[...] = jnp.where((token >= lo) & (token < hi), 0.0, -FAR).astype(BF16)


def list_tiles(tiles, starts, firsts, g, is_v):
    homes = RB // 64

    def value_token(f):
        c = f // 96
        i = f - c * 96
        return HOME * c + jnp.where(i >= 48, i + 48, i) + 48 * (g - KTYPES)

    def block(blk, count):
        first = jnp.where(is_v, value_token(blk * RB), HOME * homes * blk + 16 * g)
        last = jnp.where(
            is_v, value_token(blk * RB + RB - 1), HOME * (homes * blk + homes - 1) + HALF + 16 * g + 15
        )
        c0, c1 = 0, NCOLS
        for t, c in zip(starts, firsts):
            c0 = jnp.where(first >= t, c, c0)
        for t, c in reversed(list(zip(starts, firsts))):
            c1 = jnp.where(last < t, c, c1)
        c0 = lax.shift_left(lax.shift_right_logical(c0, 4), 4)
        for k in range(MOST_TURNS):
            tiles[count + k] = blk * 65536 + c0 + k * CB
        return count + lax.div(c1 - c0 + CB - 1, CB)

    blocks = jnp.where(is_v, NBLK, CTX * 64 // RB)
    count = jnp.int32(1)
    for blk in range(NBLK):
        count = jnp.where(blk < blocks, block(blk, count), count)
    for k in range(UNROLL + 1):
        tiles[count + k] = NCOLS
    tiles[0] = count - 1


def spot(tile, tiles):
    code = tiles[tile]
    blk, col = lax.shift_right_logical(code, 16), m16(code & 65535)
    return blk, pl.ds(pl.multiple_of(blk * RB, RB), RB), pl.ds(col, CB)


def stats_kernel(
    in_ref, out_ref, colt, cols, rowt_t, rows_t, featc, mask_t, tiles,
    rowt, rows, top_t, sum_t, top_s, sum_s, at_, as_, bt_, bs_,
):
    b, g, is_v = place()
    starts, firsts = documents(in_ref, b)
    list_tiles(tiles, starts, firsts, g, is_v)
    marks(featc, mask_t, starts, firsts, g, is_v)
    assemble(in_ref, 0, colt, rowt, rowt_t, b, g, is_v)
    assemble(in_ref, PART, cols, rows, rows_t, b, g, is_v)
    for ref in (top_t, top_s):
        ref[...] = jnp.full(ref.shape, -FAR, F32)
    for ref in (sum_t, sum_s):
        ref[...] = jnp.zeros(ref.shape, F32)
    rest = jnp.zeros((WIDTH - 16, RB), BF16)
    count = tiles[0]

    models = ((colt, rowt_t, top_t, sum_t), (cols, rows_t, top_s, sum_s))

    def score(tile, k, buf):
        _, rsl, csl = spot(tile, tiles)
        c_ref, r_ref, _, _ = models[k]
        left = jnp.concatenate([c_ref[csl, :], featc[csl, :]], axis=1)
        right = jnp.concatenate([r_ref[:, rsl], mask_t[:, rsl], rest], axis=0)
        d = jnp.dot(left, right, preferred_element_type=F32)
        buf[...] = d
        return jnp.max(d.reshape(CB // 8, 8, RB), axis=0)

    def gather(tile, k, buf, high):
        blk = spot(tile, tiles)[0]
        _, _, top, total = models[k]
        old = top[blk]
        new = jnp.maximum(old, high)
        acc = total[blk] * jnp.exp2((old - new) * C2)
        for q in range(CB // 16):
            e = jnp.exp2((buf[q * 16 : q * 16 + 16, :].reshape(16 // 8, 8, RB) - new[None]) * C2)
            acc += jnp.sum(e, axis=0)
        total[blk] = acc
        top[blk] = new

    def turn(i, highs):
        ht, hs = highs
        for k in range(UNROLL):
            a, b = ((at_, as_), (bt_, bs_)) if k % 2 == 0 else ((bt_, bs_), (at_, as_))
            nt = score(UNROLL * i + k + 2, 0, b[0])
            gather(UNROLL * i + k + 1, 0, a[0], ht)
            ns = score(UNROLL * i + k + 2, 1, b[1])
            gather(UNROLL * i + k + 1, 1, a[1], hs)
            ht, hs = nt, ns
        return ht, hs

    lax.fori_loop(0, (count + UNROLL - 1) // UNROLL, turn, (score(1, 0, at_), score(1, 1, as_)))
    out_ref[...] = jnp.zeros(out_ref.shape, F32)
    for k, (top, total) in enumerate(((top_t, sum_t), (top_s, sum_s))):
        for blk in range(NBLK):
            t = top[blk]
            most = jnp.max(t, axis=0, keepdims=True)
            out_ref[2 * k, blk : blk + 1, :] = most
            out_ref[2 * k + 1, blk : blk + 1, :] = jnp.sum(
                total[blk] * jnp.exp2((t - most) * C2), axis=0, keepdims=True
            )


def in_three(x):
    high = x.astype(BF16).astype(F32)
    mid = (x - high).astype(BF16).astype(F32)
    low = x - high - mid
    row = lax.broadcasted_iota(jnp.int32, (16, x.shape[1]), 0)
    return jnp.where(row == 0, high, jnp.where(row == 1, mid, jnp.where(row == 2, low, 0.0))).astype(BF16)


def grads_kernel(
    colt, cols, rowt_t, rows_t, featc, mask_t, tiles, mine, other, out_ref,
    lset, lses, rgt, cg, rgf, at_, as_, bt_, bs_, ga_, gb_,
):
    b, g, is_v = place()
    count = tiles[0]
    cg[...] = jnp.zeros(cg.shape, F32)
    gb_[...] = jnp.zeros(gb_.shape, BF16)
    rgt[...] = jnp.zeros(rgt.shape, F32)

    lses2 = []
    for k in (0, 2):
        top = jnp.maximum(mine[k], other[k])
        total = mine[k + 1] * jnp.exp2((mine[k] - top) * C2) + other[k + 1] * jnp.exp2((other[k] - top) * C2)
        lses2.append(top + jnp.log2(total) * (1.0 / C2))
    for blk in range(NBLK):
        at = slice(blk * RB, blk * RB + RB)
        lset[:, at] = in_three(-lses2[0][blk : blk + 1])
        lses[:, at] = in_three(-lses2[1][blk : blk + 1])
    rest = jnp.zeros((WIDTH - 32, RB), BF16)

    def scores(tile, bufs):
        _, rsl, csl = spot(tile, tiles)
        for c_ref, r_ref, lse, buf in ((colt, rowt_t, lset, bufs[0]), (cols, rows_t, lses, bufs[1])):
            left = jnp.concatenate([c_ref[csl, :], featc[csl, :]], axis=1)
            right = jnp.concatenate([r_ref[:, rsl], mask_t[:, rsl], lse[:, rsl], rest], axis=0)
            buf[...] = jnp.dot(left, right, preferred_element_type=F32)

    def differ(bufs, diff, kl):
        for q in range(0, CB, 16):
            xt, xs = bufs[0][q : q + 16, :], bufs[1][q : q + 16, :]
            pt = jnp.exp2(xt * C2)
            diff[q : q + 16, :] = (jnp.exp2(xs * C2) - pt).astype(BF16)
            kl += jnp.sum((pt * (xt - xs)).reshape(16 // 8, 8, RB), axis=0)
        return kl

    def spread(tile, diff):
        blk, rsl, csl = spot(tile, tiles)
        cg[csl, :] += lax.dot_general(diff[...], rows_t[:, rsl], NT, preferred_element_type=F32)
        rgt[blk] += lax.dot_general(cols[csl, :], diff[...], (((0,), (0,)), ((), ())), preferred_element_type=F32)

    even, odd = (at_, as_), (bt_, bs_)
    turns = (count + UNROLL - 1) // UNROLL

    def turn(i, kl):
        for k in range(UNROLL):
            a, b = (even, odd) if k % 2 == 0 else (odd, even)
            da, db = (ga_, gb_) if k % 2 == 0 else (gb_, ga_)
            scores(UNROLL * i + k + 2, b)
            spread(jnp.where(i == 0, count + 1, UNROLL * i) if k == 0 else UNROLL * i + k, db)
            kl = differ(a, da, kl)
        return kl

    scores(1, even)
    kl = lax.fori_loop(0, turns, turn, jnp.zeros((8, RB), F32))
    spread(UNROLL * turns, gb_)
    pieces = in_three(jnp.full((1, WIDTH), SCALE, F32) * jnp.sum(kl))

    for blk in range(NBLK):
        rgf[blk * RB : blk * RB + RB, :] = rgt[blk].T

    @pl.when(jnp.logical_not(is_v))
    def _():
        def one_home(c, _):
            r = c * 64
            cg[pl.ds(m16(c * HALF + 16 * g), 16), :] += rgf[pl.ds(m16(r + 32 + 16 * b), 16), :]
            out_ref[c, 96:128, :] = (rgf[pl.ds(m16(r), 32), :] * SCALE).astype(BF16)
            out_ref[c, 128:144, :] = (rgf[pl.ds(m16(r + 32 + 16 * (1 - b)), 16), :] * SCALE).astype(BF16)
            return 0

        lax.fori_loop(0, CTX, one_home, 0, unroll=4)

    @pl.when(is_v)
    def _():
        gv = g - KTYPES

        def one_home(c, _):
            r = c * 96
            cg[pl.ds(m16(c * HALF + 48 * gv), 48), :] += rgf[pl.ds(m16(r + 48 * b), 48), :]
            out_ref[c, 96:144, :] = (rgf[pl.ds(m16(r + 48 * (1 - b)), 48), :] * SCALE).astype(BF16)
            return 0

        lax.fori_loop(0, CTX, one_home, 0, unroll=4)

    def columns(c, _):
        out_ref[c, 0:HALF, :] = (cg[pl.ds(m16(c * HALF), HALF), :] * SCALE).astype(BF16)
        out_ref[c, 144:, :] = pieces[:EXTRA]
        return 0

    lax.fori_loop(0, CTX, columns, 0, unroll=4)


def loss_kernel(in_ref, loss_ref):
    total = jnp.sum(in_ref[:, 144:, :].astype(F32), axis=0)
    loss_ref[...] = jnp.sum(total, axis=0, keepdims=True)


def sum_kernel(in_ref, out_ref):
    def at(h, g, b):
        return (h * 8 + g) * 2 + b

    def part(d, lo, n):
        return in_ref[d, lo : lo + n, :].astype(F32)

    for h in range(2):
        lanes = slice(h * WIDTH, (h + 1) * WIDTH)
        for g in range(KTYPES):
            q = part(at(h, g, 0), 96, 32) + part(at(h, g, 1), 96, 32)
            out_ref[0, 16 * g : 16 * g + 16, lanes] = q[:16]
            out_ref[0, HALF + 16 * g : HALF + 16 * g + 16, lanes] = q[16:]
        for b in range(2):
            for g in range(KTYPES):
                own = part(at(h, g, 1 - b), 128, 16)
                for k in range(KTYPES):
                    own += part(at(h, k, b), 16 * g, 16)
                out_ref[1, HALF * b + 16 * g : HALF * b + 16 * g + 16, lanes] = own
            for v in range(2):
                own = part(at(h, KTYPES + v, 1 - b), 96, 48)
                for k in range(2):
                    own += part(at(h, KTYPES + k, b), 48 * v, 48)
                out_ref[2, HALF * b + 48 * v : HALF * b + 48 * v + 48, lanes] = own


def bf16(*shape):
    return jax.ShapeDtypeStruct(shape, BF16)


def pack(teacher, student, segment_ids):
    return pl.pallas_call(
        pack_kernel,
        out_shape=bf16(CTX, 2 * PART + EXTRA, WIDTH),
        compiler_params=params(),
        name="pack",
    )(teacher, student, segment_ids.reshape(1, HOME))


TILE = pltpu.VMEM((CB, RB), F32)


def row_stats(held, name="stats"):
    in_vmem, in_smem = pl.BlockSpec(memory_space=pltpu.VMEM), pl.BlockSpec(memory_space=pltpu.SMEM)
    return pl.pallas_call(
        stats_kernel,
        out_shape=[
            jax.ShapeDtypeStruct((4, 16, RB), F32),
            bf16(PADC, WIDTH), bf16(PADC, WIDTH), bf16(WIDTH, ROWS), bf16(WIDTH, ROWS), bf16(PADC, WIDTH), bf16(16, ROWS),
            jax.ShapeDtypeStruct((MAXT,), jnp.int32),
        ],
        out_specs=[in_vmem] * 7 + [in_smem],
        scratch_shapes=[pltpu.VMEM((ROWS, WIDTH), BF16)] * 2 + [pltpu.VMEM((NBLK, 8, RB), F32)] * 4 + [TILE] * 4,
        compiler_params=params(),
        name=name,
    )(held)


def grad_terms(found, other, name="grads"):
    stats, colt, cols, rowt_t, rows_t, featc, mask_t, tiles = found
    in_vmem, in_smem = pl.BlockSpec(memory_space=pltpu.VMEM), pl.BlockSpec(memory_space=pltpu.SMEM)
    return pl.pallas_call(
        grads_kernel,
        out_shape=bf16(CTX, OUT_ROWS, WIDTH),
        in_specs=[in_vmem] * 6 + [in_smem] + [in_vmem] * 2,
        scratch_shapes=[
            pltpu.VMEM((16, ROWS), BF16),
            pltpu.VMEM((16, ROWS), BF16),
            pltpu.VMEM((NBLK, WIDTH, RB), F32),
            pltpu.VMEM((PADC, WIDTH), F32),
            pltpu.VMEM((ROWS, WIDTH), F32),
        ]
        + [TILE] * 4
        + [pltpu.VMEM((CB, RB), BF16)] * 2,
        compiler_params=params(),
        name=name,
    )(colt, cols, rowt_t, rows_t, featc, mask_t, tiles, stats, other)


def swap(stats):
    return lax.ppermute(stats, "ctx", [(i, i ^ 1) for i in range(CTX)])


def shards(teacher_qkv, student_qkv, segment_ids):
    teacher = jnp.transpose(teacher_qkv, (1, 0, 2))
    student = jnp.transpose(student_qkv, (1, 0, 2))
    held = lax.all_to_all(pack(teacher, student, segment_ids), "ctx", 0, 0, tiled=True)
    found = row_stats(held)
    other = swap(found[0])
    terms = grad_terms(found, other)
    back = lax.all_to_all(terms, "ctx", 0, 0, tiled=True)
    part = pl.pallas_call(
        loss_kernel,
        out_shape=jax.ShapeDtypeStruct((1, WIDTH), F32),
        compiler_params=params(),
        name="loss_part",
    )(back)
    peers = [lax.ppermute(part, "tp", [(i, i ^ k) for i in range(4)]) for k in (1, 2, 3)]
    grad = pl.pallas_call(
        sum_kernel,
        out_shape=jax.ShapeDtypeStruct((3, HOME, 2 * WIDTH), F32),
        compiler_params=params(),
        cost_estimate=pl.CostEstimate(flops=10_000_000, bytes_accessed=8_000_000, transcendentals=0),
        name="home_sum",
    )(back)
    loss = ((part + peers[0]) + (peers[1] + peers[2]))[0, 0] / (CTX * HOME)
    return loss, jnp.transpose(grad, (1, 0, 2))


def solution(mesh):
    return jax.shard_map(
        shards,
        mesh=mesh,
        in_specs=(P("ctx", None, "tp"), P("ctx", None, "tp"), P("ctx")),
        out_specs=(P(), P("ctx", None, "tp")),
        check_vma=False,
    )
```

```python
import math

import jax
import jax.numpy as jnp
from jax import lax
from jax.experimental import pallas as pl
from jax.experimental.pallas import tpu as pltpu
from jax.sharding import PartitionSpec as P

WIDTH = 128
CTX = 32
HOME = 192
HALF = 96
LAST = 5
KTYPES = 6
SCALE = WIDTH**-0.5
LOG2E = math.log2(math.e)
C2 = SCALE * LOG2E
FAR = 2.0**100
NCOLS = CTX * HALF
ROWS = CTX * HALF
RB = 256
CB = 256
NBLK = ROWS // RB
PADC = NCOLS + 256
UNROLL, GRAD_UNROLL = 4, 6
MOST_TURNS = NCOLS // CB + 1
MAXT = 256
PART = HALF + 48
EXTRA = 8
OUT_ROWS = HALF + 48 + EXTRA
F32 = jnp.float32
BF16 = jnp.bfloat16
NT = (((1,), (1,)), ((), ()))


def params(mib=24, **kw):
    return pltpu.CompilerParams(vmem_limit_bytes=mib * 1024 * 1024, **kw)


def pack_kernel(t_ref, s_ref, seg_ref, out_ref):
    seg = jnp.broadcast_to(seg_ref[...], (EXTRA, HOME))
    step = lax.broadcasted_iota(jnp.int32, (EXTRA, HOME), 0)
    counts = jnp.sum(jnp.where(seg < step, 1.0, 0.0), axis=1, keepdims=True)
    counts = jnp.broadcast_to(counts, (EXTRA, WIDTH)).astype(BF16)
    for d in range(CTX):
        b, g, h = d % 2, (d // 2) % 8, d // 16
        lanes = slice(h * WIDTH, (h + 1) * WIDTH)
        for k, ref in enumerate((t_ref, s_ref)):
            o = k * PART
            part = 1 if g < KTYPES else 2
            out_ref[d, o : o + HALF, :] = ref[part, HALF * b : HALF * b + HALF, lanes]
            o += HALF
            if g < KTYPES:
                out_ref[d, o : o + 16, :] = ref[0, 16 * g : 16 * g + 16, lanes]
                out_ref[d, o + 16 : o + 32, :] = ref[0, HALF + 16 * g : HALF + 16 * g + 16, lanes]
                at = HALF * (1 - b) + 16 * g
                out_ref[d, o + 32 : o + 48, :] = ref[1, at : at + 16, lanes]
            else:
                at = HALF * (1 - b) + 48 * (g - KTYPES)
                out_ref[d, o : o + 48, :] = ref[2, at : at + 48, lanes]
        out_ref[d, 2 * PART :, :] = counts


def place():
    role = lax.axis_index("ctx")
    b = lax.rem(role, 2)
    g = lax.rem(role // 2, 8)
    return b, g, g >= KTYPES


def m16(x):
    return pl.multiple_of(x, 16)


def assemble(in_ref, o, cols, rows, rows_t, b, g, is_v):
    cols[NCOLS:, :] = jnp.zeros((PADC - NCOLS, WIDTH), BF16)

    def columns(c, _):
        cols[pl.ds(m16(c * HALF), HALF), :] = in_ref[c, o : o + HALF, :]
        return 0

    lax.fori_loop(0, CTX, columns, 0, unroll=4)

    @pl.when(jnp.logical_not(is_v))
    def _():
        def one(c, _):
            r = c * 64
            rows[pl.ds(m16(r), 32), :] = in_ref[c, o + 96 : o + 128, :]
            rows[pl.ds(m16(r + 32 + 16 * (1 - b)), 16), :] = in_ref[c, o + 128 : o + 144, :]
            rows[pl.ds(m16(r + 32 + 16 * b), 16), :] = in_ref[c, pl.ds(m16(o + 16 * g), 16), :]
            return 0

        lax.fori_loop(0, CTX, one, 0, unroll=4)

    @pl.when(is_v)
    def _():
        gv = g - KTYPES

        def one(c, _):
            r = c * 96
            rows[pl.ds(m16(r + 48 * (1 - b)), 48), :] = in_ref[c, o + 96 : o + 144, :]
            rows[pl.ds(m16(r + 48 * b), 48), :] = in_ref[c, pl.ds(m16(o + 48 * gv), 48), :]
            return 0

        lax.fori_loop(0, CTX, one, 0, unroll=4)

    for k in range(ROWS // 128):
        at = slice(k * 128, k * 128 + 128)
        rows_t[:, at] = rows[at, :].T


def documents(in_ref, b):
    total = jnp.sum(in_ref[:, 2 * PART :, :].astype(F32), axis=0)
    starts, firsts = [], []
    for d in range(1, LAST + 1):
        t = jnp.max(total[d : d + 1, :]).astype(jnp.int32)
        home = t // HOME
        starts.append(t)
        firsts.append(home * HALF + jnp.clip(t - home * HOME - HALF * b, 0, HALF))
    return starts, firsts


def marks(featc, mask_t, starts, firsts, g, is_v):
    def edges(at, points, rest_lo, rest_hi):
        lo = jnp.full(at.shape, rest_lo, jnp.int32)
        hi = jnp.full(at.shape, rest_hi, jnp.int32)
        for s in range(len(points) - 1):
            lo = jnp.where(at == s, points[s], lo)
            hi = jnp.where(at == s, points[s + 1], hi)
        return lo, hi

    lane = lax.broadcasted_iota(jnp.int32, (1, WIDTH), 1)
    lo, hi = edges(lane, [0, *firsts, NCOLS, PADC], 0, 0)
    ones = (lane >= 16) & (lane < 19)
    lo, hi = jnp.where(ones, 0, lo), jnp.where(ones, PADC, hi)
    at = lax.broadcasted_iota(jnp.int32, (128, WIDTH), 0)

    def column_block(k, _):
        j = at + k * 128
        inside = (j >= lo) & (j < hi)
        featc[pl.ds(pl.multiple_of(k * 128, 128), 128), :] = jnp.where(inside, 1.0, 0.0).astype(BF16)
        return 0

    lax.fori_loop(0, PADC // 128, column_block, 0, unroll=True)
    tokens = CTX * HOME
    entry = lax.broadcasted_iota(jnp.int32, (16, 1), 0)
    lo, hi = edges(entry, [0, *starts, tokens], -1, 2 * tokens)
    lo = jnp.where(entry == LAST + 1, 2 * tokens, lo)
    f = lax.broadcasted_iota(jnp.int32, (1, ROWS), 1)
    i, c = f & 63, f >> 6
    key_token = HOME * c + HALF * ((i >> 4) & 1) + (i & 15) + 16 * g
    c = ((f.astype(F32) + 0.5) * (1.0 / 96.0)).astype(jnp.int32)
    i = f - 96 * c
    value_token = HOME * c + i + jnp.where(i >= 48, 48, 0) + 48 * (g - KTYPES)
    token = jnp.where(is_v, value_token, key_token)
    mask_t[...] = jnp.where((token >= lo) & (token < hi), 0.0, -FAR).astype(BF16)


def list_tiles(tiles, starts, firsts, g, is_v):
    homes = RB // 64

    def value_token(f):
        c = f // 96
        i = f - c * 96
        return HOME * c + jnp.where(i >= 48, i + 48, i) + 48 * (g - KTYPES)

    def block(blk, count):
        first = jnp.where(is_v, value_token(blk * RB), HOME * homes * blk + 16 * g)
        last = jnp.where(
            is_v, value_token(blk * RB + RB - 1), HOME * (homes * blk + homes - 1) + HALF + 16 * g + 15
        )
        c0, c1 = 0, NCOLS
        for t, c in zip(starts, firsts):
            c0 = jnp.where(first >= t, c, c0)
        for t, c in reversed(list(zip(starts, firsts))):
            c1 = jnp.where(last < t, c, c1)
        c0 = lax.shift_left(lax.shift_right_logical(c0, 4), 4)
        for k in range(MOST_TURNS):
            tiles[count + k] = blk * 65536 + c0 + k * CB
        return count + lax.div(c1 - c0 + CB - 1, CB)

    blocks = jnp.where(is_v, NBLK, CTX * 64 // RB)
    count = jnp.int32(1)
    for blk in range(NBLK):
        count = jnp.where(blk < blocks, block(blk, count), count)
    for k in range(GRAD_UNROLL + 1):
        tiles[count + k] = NCOLS
    tiles[0] = count - 1


def spot(tile, tiles):
    code = tiles[tile]
    blk, col = lax.shift_right_logical(code, 16), m16(code & 65535)
    return blk, pl.ds(pl.multiple_of(blk * RB, RB), RB), pl.ds(col, CB)


def stats_kernel(
    in_ref, out_ref, colt, cols, rowt_t, rows_t, featc, mask_t, tiles,
    rowt, rows, top_t, sum_t, top_s, sum_s, at_, as_, bt_, bs_,
):
    b, g, is_v = place()
    starts, firsts = documents(in_ref, b)
    list_tiles(tiles, starts, firsts, g, is_v)
    marks(featc, mask_t, starts, firsts, g, is_v)
    assemble(in_ref, 0, colt, rowt, rowt_t, b, g, is_v)
    assemble(in_ref, PART, cols, rows, rows_t, b, g, is_v)
    for ref in (top_t, top_s):
        ref[...] = jnp.full(ref.shape, -FAR, F32)
    for ref in (sum_t, sum_s):
        ref[...] = jnp.zeros(ref.shape, F32)
    rest = jnp.zeros((WIDTH - 16, RB), BF16)
    count = tiles[0]

    models = ((colt, rowt_t, top_t, sum_t), (cols, rows_t, top_s, sum_s))

    def score(tile, k, buf):
        _, rsl, csl = spot(tile, tiles)
        c_ref, r_ref, _, _ = models[k]
        left = jnp.concatenate([c_ref[csl, :], featc[csl, :]], axis=1)
        right = jnp.concatenate([r_ref[:, rsl], mask_t[:, rsl], rest], axis=0)
        d = jnp.dot(left, right, preferred_element_type=F32)
        buf[...] = d
        return jnp.max(d.reshape(CB // 8, 8, RB), axis=0)

    def gather(tile, k, buf, high):
        blk = spot(tile, tiles)[0]
        _, _, top, total = models[k]
        old = top[blk]
        new = jnp.maximum(old, high)
        acc = total[blk] * jnp.exp2((old - new) * C2)
        for q in range(CB // 16):
            e = jnp.exp2((buf[q * 16 : q * 16 + 16, :].reshape(16 // 8, 8, RB) - new[None]) * C2)
            acc += jnp.sum(e, axis=0)
        total[blk] = acc
        top[blk] = new

    def turn(i, highs):
        ht, hs = highs
        for k in range(UNROLL):
            a, b = ((at_, as_), (bt_, bs_)) if k % 2 == 0 else ((bt_, bs_), (at_, as_))
            nt = score(UNROLL * i + k + 2, 0, b[0])
            gather(UNROLL * i + k + 1, 0, a[0], ht)
            ns = score(UNROLL * i + k + 2, 1, b[1])
            gather(UNROLL * i + k + 1, 1, a[1], hs)
            ht, hs = nt, ns
        return ht, hs

    lax.fori_loop(0, (count + UNROLL - 1) // UNROLL, turn, (score(1, 0, at_), score(1, 1, as_)))
    out_ref[...] = jnp.zeros(out_ref.shape, F32)
    for k, (top, total) in enumerate(((top_t, sum_t), (top_s, sum_s))):
        for blk in range(NBLK):
            t = top[blk]
            most = jnp.max(t, axis=0, keepdims=True)
            whole = jnp.sum(total[blk] * jnp.exp2((t - most) * C2), axis=0, keepdims=True)
            out_ref[k, blk : blk + 1, :] = most + jnp.log2(whole) * (1.0 / C2)


def in_three(x):
    high = x.astype(BF16).astype(F32)
    mid = (x - high).astype(BF16).astype(F32)
    low = x - high - mid
    row = lax.broadcasted_iota(jnp.int32, (16, x.shape[1]), 0)
    return jnp.where(row == 0, high, jnp.where(row == 1, mid, jnp.where(row == 2, low, 0.0))).astype(BF16)


def grads_kernel(
    colt, cols, rowt_t, rows_t, featc, mask_t, tiles, mine, other, out_ref,
    lset, lses, rgt, cg, rgf, at_, as_, bt_, bs_, ga_, gb_,
):
    b, g, is_v = place()
    count = tiles[0]
    cg[...] = jnp.zeros(cg.shape, F32)
    gb_[...] = jnp.zeros(gb_.shape, BF16)
    rgt[...] = jnp.zeros(rgt.shape, F32)

    lses2 = []
    for k in range(2):
        x, y = mine[k], other[k]
        top = jnp.maximum(x, y)
        lses2.append(top + jnp.log2(jnp.exp2((x - top) * C2) + jnp.exp2((y - top) * C2)) * (1.0 / C2))
    for blk in range(NBLK):
        at = slice(blk * RB, blk * RB + RB)
        lset[:, at] = in_three(-lses2[0][blk : blk + 1])
        lses[:, at] = in_three(-lses2[1][blk : blk + 1])
    rest = jnp.zeros((WIDTH - 32, RB), BF16)

    def scores(tile, bufs):
        _, rsl, csl = spot(tile, tiles)
        for c_ref, r_ref, lse, buf in ((colt, rowt_t, lset, bufs[0]), (cols, rows_t, lses, bufs[1])):
            left = jnp.concatenate([c_ref[csl, :], featc[csl, :]], axis=1)
            right = jnp.concatenate([r_ref[:, rsl], mask_t[:, rsl], lse[:, rsl], rest], axis=0)
            buf[...] = jnp.dot(left, right, preferred_element_type=F32)

    def differ(bufs, diff, kl):
        for q in range(0, CB, 16):
            xt, xs = bufs[0][q : q + 16, :], bufs[1][q : q + 16, :]
            pt = jnp.exp2(xt * C2)
            diff[q : q + 16, :] = (jnp.exp2(xs * C2) - pt).astype(BF16)
            kl += jnp.sum((pt * (xt - xs)).reshape(16 // 8, 8, RB), axis=0)
        return kl

    def spread(tile, diff):
        blk, rsl, csl = spot(tile, tiles)
        cg[csl, :] += lax.dot_general(diff[...], rows_t[:, rsl], NT, preferred_element_type=F32)
        rgt[blk] += lax.dot_general(cols[csl, :], diff[...], (((0,), (0,)), ((), ())), preferred_element_type=F32)

    even, odd = (at_, as_), (bt_, bs_)
    turns = (count + GRAD_UNROLL - 1) // GRAD_UNROLL

    def turn(i, kl):
        for k in range(GRAD_UNROLL):
            a, b = (even, odd) if k % 2 == 0 else (odd, even)
            da, db = (ga_, gb_) if k % 2 == 0 else (gb_, ga_)
            scores(GRAD_UNROLL * i + k + 2, b)
            spread(jnp.where(i == 0, count + 1, GRAD_UNROLL * i) if k == 0 else GRAD_UNROLL * i + k, db)
            kl = differ(a, da, kl)
        return kl

    scores(1, even)
    kl = lax.fori_loop(0, turns, turn, jnp.zeros((8, RB), F32))
    spread(GRAD_UNROLL * turns, gb_)
    pieces = in_three(jnp.full((1, WIDTH), SCALE, F32) * jnp.sum(kl))

    for blk in range(NBLK):
        rgf[blk * RB : blk * RB + RB, :] = rgt[blk].T

    @pl.when(jnp.logical_not(is_v))
    def _():
        def one_home(c, _):
            r = c * 64
            cg[pl.ds(m16(c * HALF + 16 * g), 16), :] += rgf[pl.ds(m16(r + 32 + 16 * b), 16), :]
            out_ref[c, 96:128, :] = (rgf[pl.ds(m16(r), 32), :] * SCALE).astype(BF16)
            out_ref[c, 128:144, :] = (rgf[pl.ds(m16(r + 32 + 16 * (1 - b)), 16), :] * SCALE).astype(BF16)
            return 0

        lax.fori_loop(0, CTX, one_home, 0, unroll=4)

    @pl.when(is_v)
    def _():
        gv = g - KTYPES

        def one_home(c, _):
            r = c * 96
            cg[pl.ds(m16(c * HALF + 48 * gv), 48), :] += rgf[pl.ds(m16(r + 48 * b), 48), :]
            out_ref[c, 96:144, :] = (rgf[pl.ds(m16(r + 48 * (1 - b)), 48), :] * SCALE).astype(BF16)
            return 0

        lax.fori_loop(0, CTX, one_home, 0, unroll=4)

    def columns(c, _):
        out_ref[c, 0:HALF, :] = (cg[pl.ds(m16(c * HALF), HALF), :] * SCALE).astype(BF16)
        out_ref[c, 144:, :] = pieces[:EXTRA]
        return 0

    lax.fori_loop(0, CTX, columns, 0, unroll=4)


def loss_kernel(in_ref, loss_ref):
    total = jnp.sum(in_ref[:, 144:, :].astype(F32), axis=0)
    loss_ref[...] = jnp.sum(total, axis=0, keepdims=True)


def sum_kernel(in_ref, out_ref):
    def at(h, g, b):
        return (h * 8 + g) * 2 + b

    def part(d, lo, n):
        return in_ref[d, lo : lo + n, :].astype(F32)

    for h in range(2):
        lanes = slice(h * WIDTH, (h + 1) * WIDTH)
        for g in range(KTYPES):
            q = part(at(h, g, 0), 96, 32) + part(at(h, g, 1), 96, 32)
            out_ref[0, 16 * g : 16 * g + 16, lanes] = q[:16]
            out_ref[0, HALF + 16 * g : HALF + 16 * g + 16, lanes] = q[16:]
        for b in range(2):
            for g in range(KTYPES):
                own = part(at(h, g, 1 - b), 128, 16)
                for k in range(KTYPES):
                    own += part(at(h, k, b), 16 * g, 16)
                out_ref[1, HALF * b + 16 * g : HALF * b + 16 * g + 16, lanes] = own
            for v in range(2):
                own = part(at(h, KTYPES + v, 1 - b), 96, 48)
                for k in range(2):
                    own += part(at(h, KTYPES + k, b), 48 * v, 48)
                out_ref[2, HALF * b + 48 * v : HALF * b + 48 * v + 48, lanes] = own


def bf16(*shape):
    return jax.ShapeDtypeStruct(shape, BF16)


def pack(teacher, student, segment_ids):
    return pl.pallas_call(
        pack_kernel,
        out_shape=bf16(CTX, 2 * PART + EXTRA, WIDTH),
        compiler_params=params(),
        name="pack",
    )(teacher, student, segment_ids.reshape(1, HOME))


TILE = pltpu.VMEM((CB, RB), F32)


def row_stats(held, name="stats"):
    in_vmem, in_smem = pl.BlockSpec(memory_space=pltpu.VMEM), pl.BlockSpec(memory_space=pltpu.SMEM)
    return pl.pallas_call(
        stats_kernel,
        out_shape=[
            jax.ShapeDtypeStruct((2, 16, RB), F32),
            bf16(PADC, WIDTH), bf16(PADC, WIDTH), bf16(WIDTH, ROWS), bf16(WIDTH, ROWS), bf16(PADC, WIDTH), bf16(16, ROWS),
            jax.ShapeDtypeStruct((MAXT,), jnp.int32),
        ],
        out_specs=[in_vmem] * 7 + [in_smem],
        scratch_shapes=[pltpu.VMEM((ROWS, WIDTH), BF16)] * 2 + [pltpu.VMEM((NBLK, 8, RB), F32)] * 4 + [TILE] * 4,
        compiler_params=params(),
        name=name,
    )(held)


def grad_terms(found, other, name="grads"):
    stats, colt, cols, rowt_t, rows_t, featc, mask_t, tiles = found
    in_vmem, in_smem = pl.BlockSpec(memory_space=pltpu.VMEM), pl.BlockSpec(memory_space=pltpu.SMEM)
    return pl.pallas_call(
        grads_kernel,
        out_shape=bf16(CTX, OUT_ROWS, WIDTH),
        in_specs=[in_vmem] * 6 + [in_smem] + [in_vmem] * 2,
        scratch_shapes=[
            pltpu.VMEM((16, ROWS), BF16),
            pltpu.VMEM((16, ROWS), BF16),
            pltpu.VMEM((NBLK, WIDTH, RB), F32),
            pltpu.VMEM((PADC, WIDTH), F32),
            pltpu.VMEM((ROWS, WIDTH), F32),
        ]
        + [TILE] * 4
        + [pltpu.VMEM((CB, RB), BF16)] * 2,
        compiler_params=params(),
        name=name,
    )(colt, cols, rowt_t, rows_t, featc, mask_t, tiles, stats, other)


def swap(stats):
    return lax.ppermute(stats, "ctx", [(i, i ^ 1) for i in range(CTX)])


def shards(teacher_qkv, student_qkv, segment_ids):
    teacher = jnp.transpose(teacher_qkv, (1, 0, 2))
    student = jnp.transpose(student_qkv, (1, 0, 2))
    held = lax.all_to_all(pack(teacher, student, segment_ids), "ctx", 0, 0, tiled=True)
    found = row_stats(held)
    other = swap(found[0])
    terms = grad_terms(found, other)
    back = lax.all_to_all(terms, "ctx", 0, 0, tiled=True)
    part = pl.pallas_call(
        loss_kernel,
        out_shape=jax.ShapeDtypeStruct((1, WIDTH), F32),
        compiler_params=params(),
        name="loss_part",
    )(back)
    peers = [lax.ppermute(part, "tp", [(i, i ^ k) for i in range(4)]) for k in (1, 2, 3)]
    grad = pl.pallas_call(
        sum_kernel,
        out_shape=jax.ShapeDtypeStruct((3, HOME, 2 * WIDTH), F32),
        compiler_params=params(),
        cost_estimate=pl.CostEstimate(flops=10_000_000, bytes_accessed=8_000_000, transcendentals=0),
        name="home_sum",
    )(back)
    loss = ((part + peers[0]) + (peers[1] + peers[2]))[0, 0] / (CTX * HOME)
    return loss, jnp.transpose(grad, (1, 0, 2))


def solution(mesh):
    return jax.shard_map(
        shards,
        mesh=mesh,
        in_specs=(P("ctx", None, "tp"), P("ctx", None, "tp"), P("ctx")),
        out_specs=(P(), P("ctx", None, "tp")),
        check_vma=False,
    )
```

```python
import math

import jax
import jax.numpy as jnp
from jax import lax
from jax.experimental import pallas as pl
from jax.experimental.pallas import tpu as pltpu
from jax.sharding import PartitionSpec as P

WIDTH = 128
CTX = 32
HOME = 192
HALF = 96
LAST = 5
KTYPES = 6
SCALE = WIDTH**-0.5
LOG2E = math.log2(math.e)
C2 = SCALE * LOG2E
FAR = 2.0**100
NCOLS = CTX * HALF
ROWS = CTX * HALF
RB = 256
CB = 256
NBLK = ROWS // RB
PADC = NCOLS + 256
UNROLL, GRAD_UNROLL = 4, 6
MOST_TURNS = NCOLS // CB + 1
MAXT = 256
PART = HALF + 48
EXTRA = 8
OUT_ROWS = HALF + 48 + EXTRA
F32 = jnp.float32
BF16 = jnp.bfloat16
NT = (((1,), (1,)), ((), ()))


def params(mib=24, **kw):
    return pltpu.CompilerParams(vmem_limit_bytes=mib * 1024 * 1024, **kw)


def pack_kernel(t_ref, s_ref, seg_ref, out_ref):
    seg = jnp.broadcast_to(seg_ref[...], (EXTRA, HOME))
    step = lax.broadcasted_iota(jnp.int32, (EXTRA, HOME), 0)
    counts = jnp.sum(jnp.where(seg < step, 1.0, 0.0), axis=1, keepdims=True)
    counts = jnp.broadcast_to(counts, (EXTRA, WIDTH)).astype(BF16)
    for d in range(CTX):
        b, g, h = d % 2, (d // 2) % 8, d // 16
        lanes = slice(h * WIDTH, (h + 1) * WIDTH)
        for k, ref in enumerate((t_ref, s_ref)):
            o = k * PART
            part = 1 if g < KTYPES else 2
            out_ref[d, o : o + HALF, :] = ref[part, HALF * b : HALF * b + HALF, lanes]
            o += HALF
            if g < KTYPES:
                out_ref[d, o : o + 16, :] = ref[0, 16 * g : 16 * g + 16, lanes]
                out_ref[d, o + 16 : o + 32, :] = ref[0, HALF + 16 * g : HALF + 16 * g + 16, lanes]
                at = HALF * (1 - b) + 16 * g
                out_ref[d, o + 32 : o + 48, :] = ref[1, at : at + 16, lanes]
            else:
                at = HALF * (1 - b) + 48 * (g - KTYPES)
                out_ref[d, o : o + 48, :] = ref[2, at : at + 48, lanes]
        out_ref[d, 2 * PART :, :] = counts


def place():
    role = lax.axis_index("ctx")
    b = lax.rem(role, 2)
    g = lax.rem(role // 2, 8)
    return b, g, g >= KTYPES


def m16(x):
    return pl.multiple_of(x, 16)


def assemble(in_ref, o, cols, rows, rows_t, b, g, is_v):
    cols[NCOLS:, :] = jnp.zeros((PADC - NCOLS, WIDTH), BF16)

    def columns(c, _):
        cols[pl.ds(m16(c * HALF), HALF), :] = in_ref[c, o : o + HALF, :]
        return 0

    lax.fori_loop(0, CTX, columns, 0, unroll=4)

    @pl.when(jnp.logical_not(is_v))
    def _():
        def one(c, _):
            r = c * 64
            rows[pl.ds(m16(r), 32), :] = in_ref[c, o + 96 : o + 128, :]
            rows[pl.ds(m16(r + 32 + 16 * (1 - b)), 16), :] = in_ref[c, o + 128 : o + 144, :]
            rows[pl.ds(m16(r + 32 + 16 * b), 16), :] = in_ref[c, pl.ds(m16(o + 16 * g), 16), :]
            return 0

        lax.fori_loop(0, CTX, one, 0, unroll=4)

    @pl.when(is_v)
    def _():
        gv = g - KTYPES

        def one(c, _):
            r = c * 96
            rows[pl.ds(m16(r + 48 * (1 - b)), 48), :] = in_ref[c, o + 96 : o + 144, :]
            rows[pl.ds(m16(r + 48 * b), 48), :] = in_ref[c, pl.ds(m16(o + 48 * gv), 48), :]
            return 0

        lax.fori_loop(0, CTX, one, 0, unroll=4)

    for k in range(ROWS // 128):
        at = slice(k * 128, k * 128 + 128)
        rows_t[:, at] = rows[at, :].T


def documents(in_ref, b):
    total = jnp.sum(in_ref[:, 2 * PART :, :].astype(F32), axis=0)
    starts, firsts = [], []
    for d in range(1, LAST + 1):
        t = jnp.max(total[d : d + 1, :]).astype(jnp.int32)
        home = t // HOME
        starts.append(t)
        firsts.append(home * HALF + jnp.clip(t - home * HOME - HALF * b, 0, HALF))
    return starts, firsts


def marks(featc, mask_t, starts, firsts, g, is_v):
    def edges(at, points, rest_lo, rest_hi):
        lo = jnp.full(at.shape, rest_lo, jnp.int32)
        hi = jnp.full(at.shape, rest_hi, jnp.int32)
        for s in range(len(points) - 1):
            lo = jnp.where(at == s, points[s], lo)
            hi = jnp.where(at == s, points[s + 1], hi)
        return lo, hi

    lane = lax.broadcasted_iota(jnp.int32, (1, WIDTH), 1)
    lo, hi = edges(lane, [0, *firsts, NCOLS, PADC], 0, 0)
    ones = (lane >= 16) & (lane < 19)
    lo, hi = jnp.where(ones, 0, lo), jnp.where(ones, PADC, hi)
    at = lax.broadcasted_iota(jnp.int32, (128, WIDTH), 0)

    def column_block(k, _):
        j = at + k * 128
        inside = (j >= lo) & (j < hi)
        featc[pl.ds(pl.multiple_of(k * 128, 128), 128), :] = jnp.where(inside, 1.0, 0.0).astype(BF16)
        return 0

    lax.fori_loop(0, PADC // 128, column_block, 0, unroll=True)
    tokens = CTX * HOME
    entry = lax.broadcasted_iota(jnp.int32, (16, 1), 0)
    lo, hi = edges(entry, [0, *starts, tokens], -1, 2 * tokens)
    lo = jnp.where(entry == LAST + 1, 2 * tokens, lo)
    f = lax.broadcasted_iota(jnp.int32, (1, ROWS), 1)
    i, c = f & 63, f >> 6
    key_token = HOME * c + HALF * ((i >> 4) & 1) + (i & 15) + 16 * g
    c = ((f.astype(F32) + 0.5) * (1.0 / 96.0)).astype(jnp.int32)
    i = f - 96 * c
    value_token = HOME * c + i + jnp.where(i >= 48, 48, 0) + 48 * (g - KTYPES)
    token = jnp.where(is_v, value_token, key_token)
    mask_t[...] = jnp.where((token >= lo) & (token < hi), 0.0, -FAR).astype(BF16)


def list_tiles(tiles, starts, firsts, g, is_v):
    homes = RB // 64

    def value_token(f):
        c = f // 96
        i = f - c * 96
        return HOME * c + jnp.where(i >= 48, i + 48, i) + 48 * (g - KTYPES)

    def block(blk, count):
        first = jnp.where(is_v, value_token(blk * RB), HOME * homes * blk + 16 * g)
        last = jnp.where(
            is_v, value_token(blk * RB + RB - 1), HOME * (homes * blk + homes - 1) + HALF + 16 * g + 15
        )
        c0, c1 = 0, NCOLS
        for t, c in zip(starts, firsts):
            c0 = jnp.where(first >= t, c, c0)
        for t, c in reversed(list(zip(starts, firsts))):
            c1 = jnp.where(last < t, c, c1)
        c0 = lax.shift_left(lax.shift_right_logical(c0, 4), 4)
        for k in range(MOST_TURNS):
            tiles[count + k] = blk * 65536 + c0 + k * CB
        return count + lax.div(c1 - c0 + CB - 1, CB)

    blocks = jnp.where(is_v, NBLK, CTX * 64 // RB)
    count = jnp.int32(1)
    for blk in range(NBLK):
        count = jnp.where(blk < blocks, block(blk, count), count)
    for k in range(GRAD_UNROLL + 1):
        tiles[count + k] = NCOLS
    tiles[0] = count - 1


def spot(tile, tiles):
    code = tiles[tile]
    blk, col = lax.shift_right_logical(code, 16), m16(code & 65535)
    return blk, pl.ds(pl.multiple_of(blk * RB, RB), RB), pl.ds(col, CB)


def stats_kernel(
    in_ref, out_ref, colt, cols, rowt_t, rows_t, featc, mask_t, tiles,
    rowt, rows, top_t, sum_t, top_s, sum_s, at_, as_, bt_, bs_,
):
    b, g, is_v = place()
    starts, firsts = documents(in_ref, b)
    list_tiles(tiles, starts, firsts, g, is_v)
    marks(featc, mask_t, starts, firsts, g, is_v)
    assemble(in_ref, 0, colt, rowt, rowt_t, b, g, is_v)
    assemble(in_ref, PART, cols, rows, rows_t, b, g, is_v)
    for ref in (top_t, top_s):
        ref[...] = jnp.full(ref.shape, -FAR, F32)
    for ref in (sum_t, sum_s):
        ref[...] = jnp.zeros(ref.shape, F32)
    rest = jnp.zeros((WIDTH - 16, RB), BF16)
    count = tiles[0]

    models = ((colt, rowt_t, top_t, sum_t), (cols, rows_t, top_s, sum_s))

    def score(tile, k, buf):
        _, rsl, csl = spot(tile, tiles)
        c_ref, r_ref, _, _ = models[k]
        left = jnp.concatenate([c_ref[csl, :], featc[csl, :]], axis=1)
        right = jnp.concatenate([r_ref[:, rsl], mask_t[:, rsl], rest], axis=0)
        d = jnp.dot(left, right, preferred_element_type=F32)
        buf[...] = d
        return jnp.max(d.reshape(CB // 8, 8, RB), axis=0)

    def gather(tile, k, buf, high):
        blk = spot(tile, tiles)[0]
        _, _, top, total = models[k]
        old = top[blk]
        new = jnp.maximum(old, high)
        acc = total[blk] * jnp.exp2((old - new) * C2)
        for q in range(CB // 16):
            e = jnp.exp2((buf[q * 16 : q * 16 + 16, :].reshape(16 // 8, 8, RB) - new[None]) * C2)
            acc += jnp.sum(e, axis=0)
        total[blk] = acc
        top[blk] = new

    def turn(i, highs):
        ht, hs = highs
        for k in range(UNROLL):
            a, b = ((at_, as_), (bt_, bs_)) if k % 2 == 0 else ((bt_, bs_), (at_, as_))
            nt = score(UNROLL * i + k + 2, 0, b[0])
            gather(UNROLL * i + k + 1, 0, a[0], ht)
            ns = score(UNROLL * i + k + 2, 1, b[1])
            gather(UNROLL * i + k + 1, 1, a[1], hs)
            ht, hs = nt, ns
        return ht, hs

    lax.fori_loop(0, (count + UNROLL - 1) // UNROLL, turn, (score(1, 0, at_), score(1, 1, as_)))
    out_ref[...] = jnp.zeros(out_ref.shape, F32)
    for k, (top, total) in enumerate(((top_t, sum_t), (top_s, sum_s))):
        for blk in range(NBLK):
            t = top[blk]
            most = jnp.max(t, axis=0, keepdims=True)
            whole = jnp.sum(total[blk] * jnp.exp2((t - most) * C2), axis=0, keepdims=True)
            out_ref[k, blk : blk + 1, :] = most + jnp.log2(whole) * (1.0 / C2)


def in_three(x):
    high = x.astype(BF16).astype(F32)
    mid = (x - high).astype(BF16).astype(F32)
    low = x - high - mid
    row = lax.broadcasted_iota(jnp.int32, (16, x.shape[1]), 0)
    return jnp.where(row == 0, high, jnp.where(row == 1, mid, jnp.where(row == 2, low, 0.0))).astype(BF16)


def grads_kernel(
    colt, cols, rowt_t, rows_t, featc, mask_t, tiles, mine, other, out_ref,
    lset, lses, rgt, cg, rgf, at_, as_, bt_, bs_, ga_, gb_,
):
    b, g, is_v = place()
    count = tiles[0]
    cg[...] = jnp.zeros(cg.shape, F32)
    gb_[...] = jnp.zeros(gb_.shape, BF16)
    rgt[...] = jnp.zeros(rgt.shape, F32)

    lses2 = []
    for k in range(2):
        x, y = mine[k], other[k]
        top = jnp.maximum(x, y)
        lses2.append(top + jnp.log2(jnp.exp2((x - top) * C2) + jnp.exp2((y - top) * C2)) * (1.0 / C2))
    for blk in range(NBLK):
        at = slice(blk * RB, blk * RB + RB)
        lset[:, at] = in_three(-lses2[0][blk : blk + 1])
        lses[:, at] = in_three(-lses2[1][blk : blk + 1])
    rest = jnp.zeros((WIDTH - 32, RB), BF16)

    def scores(tile, bufs):
        _, rsl, csl = spot(tile, tiles)
        for c_ref, r_ref, lse, buf in ((colt, rowt_t, lset, bufs[0]), (cols, rows_t, lses, bufs[1])):
            left = jnp.concatenate([c_ref[csl, :], featc[csl, :]], axis=1)
            right = jnp.concatenate([r_ref[:, rsl], mask_t[:, rsl], lse[:, rsl], rest], axis=0)
            buf[...] = jnp.dot(left, right, preferred_element_type=F32)

    def differ(bufs, diff, kl):
        for q in range(0, CB, 16):
            xt, xs = bufs[0][q : q + 16, :], bufs[1][q : q + 16, :]
            pt = jnp.exp2(xt * C2)
            diff[q : q + 16, :] = (jnp.exp2(xs * C2) - pt).astype(BF16)
            kl += jnp.sum((pt * (xt - xs)).reshape(16 // 8, 8, RB), axis=0)
        return kl

    def spread(tile, diff):
        blk, rsl, csl = spot(tile, tiles)
        cg[csl, :] += lax.dot_general(diff[...], rows_t[:, rsl], NT, preferred_element_type=F32)
        rgt[blk] += lax.dot_general(cols[csl, :], diff[...], (((0,), (0,)), ((), ())), preferred_element_type=F32)

    even, odd = (at_, as_), (bt_, bs_)
    turns = (count + GRAD_UNROLL - 1) // GRAD_UNROLL

    def turn(i, kl):
        for k in range(GRAD_UNROLL):
            a, b = (even, odd) if k % 2 == 0 else (odd, even)
            da, db = (ga_, gb_) if k % 2 == 0 else (gb_, ga_)
            scores(GRAD_UNROLL * i + k + 2, b)
            spread(jnp.where(i == 0, count + 1, GRAD_UNROLL * i) if k == 0 else GRAD_UNROLL * i + k, db)
            kl = differ(a, da, kl)
        return kl

    scores(1, even)
    kl = lax.fori_loop(0, turns, turn, jnp.zeros((8, RB), F32))
    spread(GRAD_UNROLL * turns, gb_)
    pieces = in_three(jnp.full((1, WIDTH), SCALE, F32) * jnp.sum(kl))

    for blk in range(NBLK):
        rgf[blk * RB : blk * RB + RB, :] = rgt[blk].T

    @pl.when(jnp.logical_not(is_v))
    def _():
        def one_home(c, _):
            r = c * 64
            cg[pl.ds(m16(c * HALF + 16 * g), 16), :] += rgf[pl.ds(m16(r + 32 + 16 * b), 16), :]
            out_ref[c, 96:128, :] = (rgf[pl.ds(m16(r), 32), :] * SCALE).astype(BF16)
            out_ref[c, 128:144, :] = (rgf[pl.ds(m16(r + 32 + 16 * (1 - b)), 16), :] * SCALE).astype(BF16)
            return 0

        lax.fori_loop(0, CTX, one_home, 0, unroll=4)

    @pl.when(is_v)
    def _():
        gv = g - KTYPES

        def one_home(c, _):
            r = c * 96
            cg[pl.ds(m16(c * HALF + 48 * gv), 48), :] += rgf[pl.ds(m16(r + 48 * b), 48), :]
            out_ref[c, 96:144, :] = (rgf[pl.ds(m16(r + 48 * (1 - b)), 48), :] * SCALE).astype(BF16)
            return 0

        lax.fori_loop(0, CTX, one_home, 0, unroll=4)

    def columns(c, _):
        out_ref[c, 0:HALF, :] = (cg[pl.ds(m16(c * HALF), HALF), :] * SCALE).astype(BF16)
        out_ref[c, 144:, :] = pieces[:EXTRA]
        return 0

    lax.fori_loop(0, CTX, columns, 0, unroll=4)


def loss_kernel(in_ref, loss_ref):
    total = jnp.sum(in_ref[:, 144:, :].astype(F32), axis=0)
    loss_ref[...] = jnp.sum(total, axis=0, keepdims=True)


def sum_kernel(in_ref, out_ref):
    def at(h, g, b):
        return (h * 8 + g) * 2 + b

    def part(d, lo, n):
        return in_ref[d, lo : lo + n, :].astype(F32)

    for h in range(2):
        lanes = slice(h * WIDTH, (h + 1) * WIDTH)
        for g in range(KTYPES):
            q = part(at(h, g, 0), 96, 32) + part(at(h, g, 1), 96, 32)
            out_ref[0, 16 * g : 16 * g + 16, lanes] = q[:16]
            out_ref[0, HALF + 16 * g : HALF + 16 * g + 16, lanes] = q[16:]
        for b in range(2):
            for g in range(KTYPES):
                own = part(at(h, g, 1 - b), 128, 16)
                for k in range(KTYPES):
                    own += part(at(h, k, b), 16 * g, 16)
                out_ref[1, HALF * b + 16 * g : HALF * b + 16 * g + 16, lanes] = own
            for v in range(2):
                own = part(at(h, KTYPES + v, 1 - b), 96, 48)
                for k in range(2):
                    own += part(at(h, KTYPES + k, b), 48 * v, 48)
                out_ref[2, HALF * b + 48 * v : HALF * b + 48 * v + 48, lanes] = own


def bf16(*shape):
    return jax.ShapeDtypeStruct(shape, BF16)


def pack(teacher, student, segment_ids):
    return pl.pallas_call(
        pack_kernel,
        out_shape=bf16(CTX, 2 * PART + EXTRA, WIDTH),
        compiler_params=params(),
        name="pack",
    )(teacher, student, segment_ids.reshape(1, HOME))


TILE = pltpu.VMEM((CB, RB), F32)


def row_stats(held, name="stats"):
    in_vmem, in_smem = pl.BlockSpec(memory_space=pltpu.VMEM), pl.BlockSpec(memory_space=pltpu.SMEM)
    return pl.pallas_call(
        stats_kernel,
        out_shape=[
            jax.ShapeDtypeStruct((2, 16, RB), F32),
            bf16(PADC, WIDTH), bf16(PADC, WIDTH), bf16(WIDTH, ROWS), bf16(WIDTH, ROWS), bf16(PADC, WIDTH), bf16(16, ROWS),
            jax.ShapeDtypeStruct((MAXT,), jnp.int32),
        ],
        out_specs=[in_vmem] * 7 + [in_smem],
        scratch_shapes=[pltpu.VMEM((ROWS, WIDTH), BF16)] * 2 + [pltpu.VMEM((NBLK, 8, RB), F32)] * 4 + [TILE] * 4,
        compiler_params=params(),
        name=name,
    )(held)


def grad_terms(found, other, name="grads"):
    stats, colt, cols, rowt_t, rows_t, featc, mask_t, tiles = found
    in_vmem, in_smem = pl.BlockSpec(memory_space=pltpu.VMEM), pl.BlockSpec(memory_space=pltpu.SMEM)
    return pl.pallas_call(
        grads_kernel,
        out_shape=bf16(CTX, OUT_ROWS, WIDTH),
        in_specs=[in_vmem] * 6 + [in_smem] + [in_vmem] * 2,
        scratch_shapes=[
            pltpu.VMEM((16, ROWS), BF16),
            pltpu.VMEM((16, ROWS), BF16),
            pltpu.VMEM((NBLK, WIDTH, RB), F32),
            pltpu.VMEM((PADC, WIDTH), F32),
            pltpu.VMEM((ROWS, WIDTH), F32),
        ]
        + [TILE] * 4
        + [pltpu.VMEM((CB, RB), BF16)] * 2,
        compiler_params=params(),
        name=name,
    )(colt, cols, rowt_t, rows_t, featc, mask_t, tiles, stats, other)


def swap(stats):
    return lax.ppermute(stats, "ctx", [(i, i ^ 1) for i in range(CTX)])


def shards(teacher_qkv, student_qkv, segment_ids):
    teacher = jnp.transpose(teacher_qkv, (1, 0, 2))
    student = jnp.transpose(student_qkv, (1, 0, 2))
    held = lax.all_to_all(pack(teacher, student, segment_ids), "ctx", 0, 0, tiled=True)
    found = row_stats(held)
    other = swap(found[0])
    terms = grad_terms(found, other)
    back = lax.all_to_all(terms, "ctx", 0, 0, tiled=True)
    part = pl.pallas_call(
        loss_kernel,
        out_shape=jax.ShapeDtypeStruct((1, WIDTH), F32),
        compiler_params=params(),
        name="loss_part",
    )(back)
    for k in (1, 2):
        part += lax.ppermute(part, "tp", [(i, i ^ k) for i in range(4)])
    grad = pl.pallas_call(
        sum_kernel,
        out_shape=jax.ShapeDtypeStruct((3, HOME, 2 * WIDTH), F32),
        compiler_params=params(),
        cost_estimate=pl.CostEstimate(flops=10_000_000, bytes_accessed=8_000_000, transcendentals=0),
        name="home_sum",
    )(back)
    loss = part[0, 0] / (CTX * HOME)
    return loss, jnp.transpose(grad, (1, 0, 2))


def solution(mesh):
    return jax.shard_map(
        shards,
        mesh=mesh,
        in_specs=(P("ctx", None, "tp"), P("ctx", None, "tp"), P("ctx")),
        out_specs=(P(), P("ctx", None, "tp")),
        check_vma=False,
    )
```

```python
import math

import jax
import jax.numpy as jnp
from jax import lax
from jax.experimental import pallas as pl
from jax.experimental.pallas import tpu as pltpu
from jax.sharding import PartitionSpec as P

WIDTH = 128
CTX = 32
HOME = 192
HALF = 96
LAST = 5
KTYPES = 6
SCALE = WIDTH**-0.5
LOG2E = math.log2(math.e)
C2 = SCALE * LOG2E
FAR = 2.0**100
NCOLS = CTX * HALF
ROWS = CTX * HALF
RB = 256
CB = 192
NBLK = ROWS // RB
PADC = NCOLS + 256
UNROLL, GRAD_UNROLL = 6, 8
MOST_TURNS = NCOLS // CB + 1
MAXT = 256
PART = HALF + 48
EXTRA = 8
OUT_ROWS = HALF + 48 + EXTRA
F32 = jnp.float32
BF16 = jnp.bfloat16
NT = (((1,), (1,)), ((), ()))


def params(mib=24, **kw):
    return pltpu.CompilerParams(vmem_limit_bytes=mib * 1024 * 1024, **kw)


def pack_kernel(t_ref, s_ref, seg_ref, out_ref):
    seg = jnp.broadcast_to(seg_ref[...], (EXTRA, HOME))
    step = lax.broadcasted_iota(jnp.int32, (EXTRA, HOME), 0)
    counts = jnp.sum(jnp.where(seg < step, 1.0, 0.0), axis=1, keepdims=True)
    counts = jnp.broadcast_to(counts, (EXTRA, WIDTH)).astype(BF16)
    for d in range(CTX):
        b, g, h = d % 2, (d // 2) % 8, d // 16
        lanes = slice(h * WIDTH, (h + 1) * WIDTH)
        for k, ref in enumerate((t_ref, s_ref)):
            o = k * PART
            part = 1 if g < KTYPES else 2
            out_ref[d, o : o + HALF, :] = ref[part, HALF * b : HALF * b + HALF, lanes]
            o += HALF
            if g < KTYPES:
                out_ref[d, o : o + 16, :] = ref[0, 16 * g : 16 * g + 16, lanes]
                out_ref[d, o + 16 : o + 32, :] = ref[0, HALF + 16 * g : HALF + 16 * g + 16, lanes]
                at = HALF * (1 - b) + 16 * g
                out_ref[d, o + 32 : o + 48, :] = ref[1, at : at + 16, lanes]
            else:
                at = HALF * (1 - b) + 48 * (g - KTYPES)
                out_ref[d, o : o + 48, :] = ref[2, at : at + 48, lanes]
        out_ref[d, 2 * PART :, :] = counts


def place():
    role = lax.axis_index("ctx")
    b = lax.rem(role, 2)
    g = lax.rem(role // 2, 8)
    return b, g, g >= KTYPES


def m16(x):
    return pl.multiple_of(x, 16)


def assemble(in_ref, o, cols, rows, rows_t, b, g, is_v):
    cols[NCOLS:, :] = jnp.zeros((PADC - NCOLS, WIDTH), BF16)

    def columns(c, _):
        cols[pl.ds(m16(c * HALF), HALF), :] = in_ref[c, o : o + HALF, :]
        return 0

    lax.fori_loop(0, CTX, columns, 0, unroll=4)

    @pl.when(jnp.logical_not(is_v))
    def _():
        def one(c, _):
            r = c * 64
            rows[pl.ds(m16(r), 32), :] = in_ref[c, o + 96 : o + 128, :]
            rows[pl.ds(m16(r + 32 + 16 * (1 - b)), 16), :] = in_ref[c, o + 128 : o + 144, :]
            rows[pl.ds(m16(r + 32 + 16 * b), 16), :] = in_ref[c, pl.ds(m16(o + 16 * g), 16), :]
            return 0

        lax.fori_loop(0, CTX, one, 0, unroll=4)

    @pl.when(is_v)
    def _():
        gv = g - KTYPES

        def one(c, _):
            r = c * 96
            rows[pl.ds(m16(r + 48 * (1 - b)), 48), :] = in_ref[c, o + 96 : o + 144, :]
            rows[pl.ds(m16(r + 48 * b), 48), :] = in_ref[c, pl.ds(m16(o + 48 * gv), 48), :]
            return 0

        lax.fori_loop(0, CTX, one, 0, unroll=4)

    for k in range(ROWS // 128):
        at = slice(k * 128, k * 128 + 128)
        rows_t[:, at] = rows[at, :].T


def documents(in_ref, b):
    total = jnp.sum(in_ref[:, 2 * PART :, :].astype(F32), axis=0)
    starts, firsts = [], []
    for d in range(1, LAST + 1):
        t = jnp.max(total[d : d + 1, :]).astype(jnp.int32)
        home = t // HOME
        starts.append(t)
        firsts.append(home * HALF + jnp.clip(t - home * HOME - HALF * b, 0, HALF))
    return starts, firsts


def marks(featc, mask_t, starts, firsts, g, is_v):
    def edges(at, points, rest_lo, rest_hi):
        lo = jnp.full(at.shape, rest_lo, jnp.int32)
        hi = jnp.full(at.shape, rest_hi, jnp.int32)
        for s in range(len(points) - 1):
            lo = jnp.where(at == s, points[s], lo)
            hi = jnp.where(at == s, points[s + 1], hi)
        return lo, hi

    lane = lax.broadcasted_iota(jnp.int32, (1, WIDTH), 1)
    lo, hi = edges(lane, [0, *firsts, NCOLS, PADC], 0, 0)
    ones = (lane >= 16) & (lane < 19)
    lo, hi = jnp.where(ones, 0, lo), jnp.where(ones, PADC, hi)
    at = lax.broadcasted_iota(jnp.int32, (128, WIDTH), 0)

    def column_block(k, _):
        j = at + k * 128
        inside = (j >= lo) & (j < hi)
        featc[pl.ds(pl.multiple_of(k * 128, 128), 128), :] = jnp.where(inside, 1.0, 0.0).astype(BF16)
        return 0

    lax.fori_loop(0, PADC // 128, column_block, 0, unroll=True)
    tokens = CTX * HOME
    entry = lax.broadcasted_iota(jnp.int32, (16, 1), 0)
    lo, hi = edges(entry, [0, *starts, tokens], -1, 2 * tokens)
    lo = jnp.where(entry == LAST + 1, 2 * tokens, lo)
    f = lax.broadcasted_iota(jnp.int32, (1, ROWS), 1)
    i, c = f & 63, f >> 6
    key_token = HOME * c + HALF * ((i >> 4) & 1) + (i & 15) + 16 * g
    c = ((f.astype(F32) + 0.5) * (1.0 / 96.0)).astype(jnp.int32)
    i = f - 96 * c
    value_token = HOME * c + i + jnp.where(i >= 48, 48, 0) + 48 * (g - KTYPES)
    token = jnp.where(is_v, value_token, key_token)
    mask_t[...] = jnp.where((token >= lo) & (token < hi), 0.0, -FAR).astype(BF16)


def list_tiles(tiles, starts, firsts, g, is_v):
    homes = RB // 64

    def value_token(f):
        c = f // 96
        i = f - c * 96
        return HOME * c + jnp.where(i >= 48, i + 48, i) + 48 * (g - KTYPES)

    def block(blk, count):
        first = jnp.where(is_v, value_token(blk * RB), HOME * homes * blk + 16 * g)
        last = jnp.where(
            is_v, value_token(blk * RB + RB - 1), HOME * (homes * blk + homes - 1) + HALF + 16 * g + 15
        )
        c0, c1 = 0, NCOLS
        for t, c in zip(starts, firsts):
            c0 = jnp.where(first >= t, c, c0)
        for t, c in reversed(list(zip(starts, firsts))):
            c1 = jnp.where(last < t, c, c1)
        c0 = lax.shift_left(lax.shift_right_logical(c0, 4), 4)
        for k in range(MOST_TURNS):
            tiles[count + k] = blk * 65536 + c0 + k * CB
        return count + lax.div(c1 - c0 + CB - 1, CB)

    blocks = jnp.where(is_v, NBLK, CTX * 64 // RB)
    count = jnp.int32(1)
    for blk in range(NBLK):
        count = jnp.where(blk < blocks, block(blk, count), count)
    for k in range(GRAD_UNROLL + 1):
        tiles[count + k] = NCOLS
    tiles[0] = count - 1


def spot(tile, tiles):
    code = tiles[tile]
    blk, col = lax.shift_right_logical(code, 16), m16(code & 65535)
    return blk, pl.ds(pl.multiple_of(blk * RB, RB), RB), pl.ds(col, CB)


def stats_kernel(
    in_ref, out_ref, colt, cols, rowt_t, rows_t, featc, mask_t, tiles,
    rowt, rows, top_t, sum_t, top_s, sum_s, at_, as_, bt_, bs_,
):
    b, g, is_v = place()
    starts, firsts = documents(in_ref, b)
    list_tiles(tiles, starts, firsts, g, is_v)
    marks(featc, mask_t, starts, firsts, g, is_v)
    assemble(in_ref, 0, colt, rowt, rowt_t, b, g, is_v)
    assemble(in_ref, PART, cols, rows, rows_t, b, g, is_v)
    for ref in (top_t, top_s):
        ref[...] = jnp.full(ref.shape, -FAR, F32)
    for ref in (sum_t, sum_s):
        ref[...] = jnp.zeros(ref.shape, F32)
    rest = jnp.zeros((WIDTH - 16, RB), BF16)
    count = tiles[0]

    models = ((colt, rowt_t, top_t, sum_t), (cols, rows_t, top_s, sum_s))

    def score(tile, k, buf):
        _, rsl, csl = spot(tile, tiles)
        c_ref, r_ref, _, _ = models[k]
        left = jnp.concatenate([c_ref[csl, :], featc[csl, :]], axis=1)
        right = jnp.concatenate([r_ref[:, rsl], mask_t[:, rsl], rest], axis=0)
        d = jnp.dot(left, right, preferred_element_type=F32)
        buf[...] = d
        return jnp.max(d.reshape(CB // 8, 8, RB), axis=0)

    def gather(tile, k, buf, high):
        blk = spot(tile, tiles)[0]
        _, _, top, total = models[k]
        old = top[blk]
        new = jnp.maximum(old, high)
        acc = total[blk] * jnp.exp2((old - new) * C2)
        for q in range(CB // 16):
            e = jnp.exp2((buf[q * 16 : q * 16 + 16, :].reshape(16 // 8, 8, RB) - new[None]) * C2)
            acc += jnp.sum(e, axis=0)
        total[blk] = acc
        top[blk] = new

    def turn(i, highs):
        ht, hs = highs
        for k in range(UNROLL):
            a, b = ((at_, as_), (bt_, bs_)) if k % 2 == 0 else ((bt_, bs_), (at_, as_))
            nt = score(UNROLL * i + k + 2, 0, b[0])
            gather(UNROLL * i + k + 1, 0, a[0], ht)
            ns = score(UNROLL * i + k + 2, 1, b[1])
            gather(UNROLL * i + k + 1, 1, a[1], hs)
            ht, hs = nt, ns
        return ht, hs

    lax.fori_loop(0, (count + UNROLL - 1) // UNROLL, turn, (score(1, 0, at_), score(1, 1, as_)))
    out_ref[...] = jnp.zeros(out_ref.shape, F32)
    for k, (top, total) in enumerate(((top_t, sum_t), (top_s, sum_s))):
        for blk in range(NBLK):
            t = top[blk]
            most = jnp.max(t, axis=0, keepdims=True)
            whole = jnp.sum(total[blk] * jnp.exp2((t - most) * C2), axis=0, keepdims=True)
            out_ref[k, blk : blk + 1, :] = most + jnp.log2(whole) * (1.0 / C2)


def in_three(x):
    high = x.astype(BF16).astype(F32)
    mid = (x - high).astype(BF16).astype(F32)
    low = x - high - mid
    row = lax.broadcasted_iota(jnp.int32, (16, x.shape[1]), 0)
    return jnp.where(row == 0, high, jnp.where(row == 1, mid, jnp.where(row == 2, low, 0.0))).astype(BF16)


def grads_kernel(
    colt, cols, rowt_t, rows_t, featc, mask_t, tiles, mine, other, out_ref,
    lset, lses, rgt, cg, rgf, at_, as_, bt_, bs_, ga_, gb_,
):
    b, g, is_v = place()
    count = tiles[0]
    cg[...] = jnp.zeros(cg.shape, F32)
    gb_[...] = jnp.zeros(gb_.shape, BF16)
    rgt[...] = jnp.zeros(rgt.shape, F32)

    lses2 = []
    for k in range(2):
        x, y = mine[k], other[k]
        top = jnp.maximum(x, y)
        lses2.append(top + jnp.log2(jnp.exp2((x - top) * C2) + jnp.exp2((y - top) * C2)) * (1.0 / C2))
    for blk in range(NBLK):
        at = slice(blk * RB, blk * RB + RB)
        lset[:, at] = in_three(-lses2[0][blk : blk + 1])
        lses[:, at] = in_three(-lses2[1][blk : blk + 1])
    rest = jnp.zeros((WIDTH - 32, RB), BF16)

    def scores(tile, bufs):
        _, rsl, csl = spot(tile, tiles)
        for c_ref, r_ref, lse, buf in ((colt, rowt_t, lset, bufs[0]), (cols, rows_t, lses, bufs[1])):
            left = jnp.concatenate([c_ref[csl, :], featc[csl, :]], axis=1)
            right = jnp.concatenate([r_ref[:, rsl], mask_t[:, rsl], lse[:, rsl], rest], axis=0)
            buf[...] = jnp.dot(left, right, preferred_element_type=F32)

    def differ(bufs, diff, kl):
        for q in range(0, CB, 16):
            xt, xs = bufs[0][q : q + 16, :], bufs[1][q : q + 16, :]
            pt = jnp.exp2(xt * C2)
            diff[q : q + 16, :] = (jnp.exp2(xs * C2) - pt).astype(BF16)
            kl += jnp.sum((pt * (xt - xs)).reshape(16 // 8, 8, RB), axis=0)
        return kl

    def spread(tile, diff):
        blk, rsl, csl = spot(tile, tiles)
        cg[csl, :] += lax.dot_general(diff[...], rows_t[:, rsl], NT, preferred_element_type=F32)
        rgt[blk] += lax.dot_general(cols[csl, :], diff[...], (((0,), (0,)), ((), ())), preferred_element_type=F32)

    even, odd = (at_, as_), (bt_, bs_)
    turns = (count + GRAD_UNROLL - 1) // GRAD_UNROLL

    def turn(i, kl):
        for k in range(GRAD_UNROLL):
            a, b = (even, odd) if k % 2 == 0 else (odd, even)
            da, db = (ga_, gb_) if k % 2 == 0 else (gb_, ga_)
            scores(GRAD_UNROLL * i + k + 2, b)
            spread(jnp.where(i == 0, count + 1, GRAD_UNROLL * i) if k == 0 else GRAD_UNROLL * i + k, db)
            kl = differ(a, da, kl)
        return kl

    scores(1, even)
    kl = lax.fori_loop(0, turns, turn, jnp.zeros((8, RB), F32))
    spread(GRAD_UNROLL * turns, gb_)
    pieces = in_three(jnp.full((1, WIDTH), SCALE, F32) * jnp.sum(kl))

    for blk in range(NBLK):
        rgf[blk * RB : blk * RB + RB, :] = rgt[blk].T

    @pl.when(jnp.logical_not(is_v))
    def _():
        def one_home(c, _):
            r = c * 64
            cg[pl.ds(m16(c * HALF + 16 * g), 16), :] += rgf[pl.ds(m16(r + 32 + 16 * b), 16), :]
            out_ref[c, 96:128, :] = (rgf[pl.ds(m16(r), 32), :] * SCALE).astype(BF16)
            out_ref[c, 128:144, :] = (rgf[pl.ds(m16(r + 32 + 16 * (1 - b)), 16), :] * SCALE).astype(BF16)
            return 0

        lax.fori_loop(0, CTX, one_home, 0, unroll=4)

    @pl.when(is_v)
    def _():
        gv = g - KTYPES

        def one_home(c, _):
            r = c * 96
            cg[pl.ds(m16(c * HALF + 48 * gv), 48), :] += rgf[pl.ds(m16(r + 48 * b), 48), :]
            out_ref[c, 96:144, :] = (rgf[pl.ds(m16(r + 48 * (1 - b)), 48), :] * SCALE).astype(BF16)
            return 0

        lax.fori_loop(0, CTX, one_home, 0, unroll=4)

    def columns(c, _):
        out_ref[c, 0:HALF, :] = (cg[pl.ds(m16(c * HALF), HALF), :] * SCALE).astype(BF16)
        out_ref[c, 144:, :] = pieces[:EXTRA]
        return 0

    lax.fori_loop(0, CTX, columns, 0, unroll=4)


def loss_kernel(in_ref, loss_ref):
    total = jnp.sum(in_ref[:, 144:, :].astype(F32), axis=0)
    loss_ref[...] = jnp.sum(total, axis=0, keepdims=True)


def sum_kernel(in_ref, out_ref):
    def at(h, g, b):
        return (h * 8 + g) * 2 + b

    def part(d, lo, n):
        return in_ref[d, lo : lo + n, :].astype(F32)

    for h in range(2):
        lanes = slice(h * WIDTH, (h + 1) * WIDTH)
        for g in range(KTYPES):
            q = part(at(h, g, 0), 96, 32) + part(at(h, g, 1), 96, 32)
            out_ref[0, 16 * g : 16 * g + 16, lanes] = q[:16]
            out_ref[0, HALF + 16 * g : HALF + 16 * g + 16, lanes] = q[16:]
        for b in range(2):
            for g in range(KTYPES):
                own = part(at(h, g, 1 - b), 128, 16)
                for k in range(KTYPES):
                    own += part(at(h, k, b), 16 * g, 16)
                out_ref[1, HALF * b + 16 * g : HALF * b + 16 * g + 16, lanes] = own
            for v in range(2):
                own = part(at(h, KTYPES + v, 1 - b), 96, 48)
                for k in range(2):
                    own += part(at(h, KTYPES + k, b), 48 * v, 48)
                out_ref[2, HALF * b + 48 * v : HALF * b + 48 * v + 48, lanes] = own


def bf16(*shape):
    return jax.ShapeDtypeStruct(shape, BF16)


def pack(teacher, student, segment_ids):
    return pl.pallas_call(
        pack_kernel,
        out_shape=bf16(CTX, 2 * PART + EXTRA, WIDTH),
        compiler_params=params(),
        name="pack",
    )(teacher, student, segment_ids.reshape(1, HOME))


TILE = pltpu.VMEM((CB, RB), F32)


def row_stats(held, name="stats"):
    in_vmem, in_smem = pl.BlockSpec(memory_space=pltpu.VMEM), pl.BlockSpec(memory_space=pltpu.SMEM)
    return pl.pallas_call(
        stats_kernel,
        out_shape=[
            jax.ShapeDtypeStruct((2, 16, RB), F32),
            bf16(PADC, WIDTH), bf16(PADC, WIDTH), bf16(WIDTH, ROWS), bf16(WIDTH, ROWS), bf16(PADC, WIDTH), bf16(16, ROWS),
            jax.ShapeDtypeStruct((MAXT,), jnp.int32),
        ],
        out_specs=[in_vmem] * 7 + [in_smem],
        scratch_shapes=[pltpu.VMEM((ROWS, WIDTH), BF16)] * 2 + [pltpu.VMEM((NBLK, 8, RB), F32)] * 4 + [TILE] * 4,
        compiler_params=params(),
        name=name,
    )(held)


def grad_terms(found, other, name="grads"):
    stats, colt, cols, rowt_t, rows_t, featc, mask_t, tiles = found
    in_vmem, in_smem = pl.BlockSpec(memory_space=pltpu.VMEM), pl.BlockSpec(memory_space=pltpu.SMEM)
    return pl.pallas_call(
        grads_kernel,
        out_shape=bf16(CTX, OUT_ROWS, WIDTH),
        in_specs=[in_vmem] * 6 + [in_smem] + [in_vmem] * 2,
        scratch_shapes=[
            pltpu.VMEM((16, ROWS), BF16),
            pltpu.VMEM((16, ROWS), BF16),
            pltpu.VMEM((NBLK, WIDTH, RB), F32),
            pltpu.VMEM((PADC, WIDTH), F32),
            pltpu.VMEM((ROWS, WIDTH), F32),
        ]
        + [TILE] * 4
        + [pltpu.VMEM((CB, RB), BF16)] * 2,
        compiler_params=params(),
        name=name,
    )(colt, cols, rowt_t, rows_t, featc, mask_t, tiles, stats, other)


def swap(stats):
    return lax.ppermute(stats, "ctx", [(i, i ^ 1) for i in range(CTX)])


def shards(teacher_qkv, student_qkv, segment_ids):
    teacher = jnp.transpose(teacher_qkv, (1, 0, 2))
    student = jnp.transpose(student_qkv, (1, 0, 2))
    held = lax.all_to_all(pack(teacher, student, segment_ids), "ctx", 0, 0, tiled=True)
    found = row_stats(held)
    other = swap(found[0])
    terms = grad_terms(found, other)
    back = lax.all_to_all(terms, "ctx", 0, 0, tiled=True)
    part = pl.pallas_call(
        loss_kernel,
        out_shape=jax.ShapeDtypeStruct((1, WIDTH), F32),
        compiler_params=params(),
        name="loss_part",
    )(back)
    for k in (1, 2):
        part += lax.ppermute(part, "tp", [(i, i ^ k) for i in range(4)])
    grad = pl.pallas_call(
        sum_kernel,
        out_shape=jax.ShapeDtypeStruct((3, HOME, 2 * WIDTH), F32),
        compiler_params=params(),
        cost_estimate=pl.CostEstimate(flops=10_000_000, bytes_accessed=8_000_000, transcendentals=0),
        name="home_sum",
    )(back)
    loss = part[0, 0] / (CTX * HOME)
    return loss, jnp.transpose(grad, (1, 0, 2))


def solution(mesh):
    return jax.shard_map(
        shards,
        mesh=mesh,
        in_specs=(P("ctx", None, "tp"), P("ctx", None, "tp"), P("ctx")),
        out_specs=(P(), P("ctx", None, "tp")),
        check_vma=False,
    )
```
